32 devices in a mesh: dp: 2 (over x), seq: 16 (over z, y, core).
Axes of the slice: x: 2, y: 2, z: 4, core: 2. Of those that a mesh axis runs over, the one named last changes fastest.
Arguments:
- tokens: bfloat16 [8192, 2048], P(('dp', 'seq'))
- cotangent: bfloat16 [8192, 2048], P(('dp', 'seq')), may hold values from -6 to 6
- attn_norm: bfloat16 [2048], P(('dp', 'seq')), may hold values from 0.25 to 1.75
- w_query: bfloat16 [2048, 2048], P(('dp', 'seq')), may hold values from -0.125 to 0.125
- w_key: bfloat16 [2048, 1024], P(('dp', 'seq')), may hold values from -0.125 to 0.125
- w_value: bfloat16 [2048, 1024], P(('dp', 'seq')), may hold values from -0.125 to 0.125
- w_output: bfloat16 [2048, 2048], P(('dp', 'seq')), may hold values from -0.5 to 0.5
- mlp_norm: bfloat16 [2048], P(('dp', 'seq')), may hold values from 0.25 to 1.75
- w_gate: bfloat16 [2048, 8192], P(('dp', 'seq')), may hold values from -0.125 to 0.125
- w_up: bfloat16 [2048, 8192], P(('dp', 'seq')), may hold values from -0.125 to 0.125
- w_down: bfloat16 [2048, 8192], P(('dp', 'seq')), may hold values from -0.0625 to 0.0625
- block_counts: int32 [2, 9], replicated, may hold values from 1 to 16, 32 in all within a row
- trims: int32 [2, 9], replicated, may hold values from 0 to 127
- block_order: int32 [2, 32], replicated, may hold values from 0 to 31, each once within a row
Outputs:
- output: bfloat16 [8192, 2048], P(('dp', 'seq'))
- input_grad: bfloat16 [8192, 2048], P(('dp', 'seq'))
- grad_attn_norm: float32 [2048], P(('dp', 'seq'))
- grad_query: float32 [2048, 2048], P(('dp', 'seq'))
- grad_key: float32 [2048, 1024], P(('dp', 'seq'))
- grad_value: float32 [2048, 1024], P(('dp', 'seq'))
- grad_output: float32 [2048, 2048], P(('dp', 'seq'))
- grad_mlp_norm: float32 [2048], P(('dp', 'seq'))
- grad_gate: float32 [2048, 8192], P(('dp', 'seq'))
- grad_up: float32 [2048, 8192], P(('dp', 'seq'))
- grad_down: float32 [2048, 8192], P(('dp', 'seq'))
- rms_stats: float32 [4, 2048], P(None, ('dp', 'seq'))
The draws below stay inside these ranges and needn't reach their ends.
Inputs may be any that keep to these rules, and one draw needn't show every extreme that they name: `block_counts`: each row sums to 32, and its largest entry is exactly 16. `block_order`: each row is a permutation of its group's blocks.
All inputs are finite; a program needn't handle non-finite values.
Results may differ from the reference program's by a relative error of at most 0.017.
Values may be sent and summed in bfloat16 or wider, within the bound.
A program may use at most 704 MiB of HBM per device.

```python
import math
import jax
import jax.numpy as jnp
import numpy as np
from jax import lax

D = 2048
H = 8
KVH = 4
HD = 256
FF = 8192
BLK = 128
MAXB = 16
NB = 32
SEQS = 9
TOKENS = 8192
N_DP = 2


def draw_tokens(key, part):
    key_base, key_rough = jax.random.split(key)
    row_index = jnp.arange(TOKENS, dtype=jnp.float32)[:, None]
    rising = jnp.exp(0.5 * math.log(3.0) * row_index / (TOKENS - 1))
    rough = jnp.exp(jax.random.uniform(key_rough, (TOKENS, 1), jnp.float32, -0.35, 0.35))
    base = jnp.clip(jax.random.normal(key_base, (TOKENS, D), jnp.float32), -6.0, 6.0)
    return (base * rising * rough).astype(jnp.bfloat16)


def plant(values, own_key, smallest, high):
    dims = values.shape
    spot = [jax.random.randint(jax.random.fold_in(own_key, axis), (), 0, dims[axis]) for axis in range(len(dims))]
    values = values.at[tuple(spot)].set(smallest)
    longest = dims.index(max(dims))
    spot[longest] = (spot[longest] + 1) % dims[longest]
    return values.at[tuple(spot)].set(high)


def block_levels(key, dims, cuts, smallest, top_value):
    loudness = 1.0
    for axis_at, shards_of in cuts:
        heights = jax.random.uniform(jax.random.fold_in(jax.random.fold_in(key, 6), axis_at), (shards_of,), jnp.float32, smallest / len(cuts), top_value / len(cuts))
        loudness = loudness * jnp.repeat(jnp.exp(heights), dims[axis_at] // shards_of).reshape((-1,) + (1,) * (len(dims) - 1 - axis_at))
    return loudness


def length_profile(count, total, reach, lean):
    portions = [(1 << 20) // math.isqrt(standing ** lean) + 1 for standing in range(2, count + 1)]
    spare, counts = total - reach - (count - 1), [1] * (count - 1)
    while spare > 0:
        free = [i for i in range(count - 1) if counts[i] < reach]
        mass, budget = sum([portions[i] for i in free]), spare
        for i in free:
            more = min(reach - counts[i], max(1, budget * portions[i] // mass), spare)
            counts[i] = counts[i] + more
            spare = spare - more
    return np.array([reach] + counts)


def uneven_parts(stream_key, number_of, total, reach, lean):
    if number_of == 2:
        one = jax.random.randint(stream_key, (), max(1, total - reach), min(reach, total - 1) + 1)
        return jnp.stack([one, total - one])
    tallies = jnp.asarray(length_profile(number_of, total, reach, lean), jnp.int32)
    twos = (number_of - 1) // 2
    giver, sink = tallies[1:1 + 2 * twos:2], tallies[2:2 + 2 * twos:2]
    margin = jnp.minimum(giver - 1, reach - sink)
    passed = jax.random.randint(jax.random.fold_in(stream_key, 1), (twos,), 0, 1 << 20) % (margin + 1)
    tallies = tallies.at[1:1 + 2 * twos:2].set(giver - passed).at[2:2 + 2 * twos:2].set(sink + passed)
    return tallies[jax.random.permutation(jax.random.fold_in(stream_key, 2), number_of)]


def centred(stream_key, dims, spread, bound, cuts=(), kind=jnp.bfloat16):
    gain = block_levels(stream_key, dims, cuts, -0.22, 0.18) if cuts else 1.0
    values = jax.random.normal(stream_key, dims, jnp.float32) * spread * gain
    return jnp.minimum(jnp.maximum(values, -bound), bound).astype(kind)


def setup_inputs(seed: int = 0) -> dict:
    arg_keys = jax.random.split(jax.random.key(seed), 15)
    return {
        "tokens": draw_tokens(jax.random.fold_in(arg_keys[14], 71), 0),
        "cotangent": centred(arg_keys[1], (TOKENS, D), 1.0, 6.0, ((0, 32),)),
        "attn_norm": jnp.clip(1.0 + 0.15 * jax.random.normal(arg_keys[2], (D,), jnp.float32), 0.25, 1.75).astype(jnp.bfloat16),
        "w_query": centred(arg_keys[3], (D, H * HD), D ** -0.5, 0.125, ((0, 32),)),
        "w_key": centred(arg_keys[4], (D, KVH * HD), D ** -0.5, 0.125, ((0, 32),)),
        "w_value": centred(arg_keys[5], (D, KVH * HD), D ** -0.5, 0.125, ((0, 32),)),
        "w_output": centred(arg_keys[6], (D, H * HD), (H * HD // 16) ** -0.5, 0.5, ((0, 32),)),
        "mlp_norm": jnp.clip(1.0 + 0.15 * jax.random.normal(arg_keys[7], (D,), jnp.float32), 0.25, 1.75).astype(jnp.bfloat16),
        "w_gate": centred(arg_keys[8], (D, FF), D ** -0.5, 0.125, ((0, 32),)),
        "w_up": centred(arg_keys[9], (D, FF), D ** -0.5, 0.125, ((0, 32),)),
        "w_down": centred(arg_keys[10], (D, FF), FF ** -0.5, 0.0625, ((0, 32),)),
        "block_counts": jax.vmap(lambda own: uneven_parts(own, SEQS, NB, MAXB, 2))(jax.random.split(arg_keys[11], N_DP)).reshape((N_DP, SEQS)).astype(jnp.int32),
        "trims": plant(jax.random.randint(arg_keys[12], (N_DP, SEQS), 0, BLK), jax.random.fold_in(arg_keys[12], 1), 0, BLK - 1).astype(jnp.int32),
        "block_order": jax.vmap(lambda own: jax.random.permutation(own, NB))(jax.random.split(arg_keys[13], N_DP)).reshape((N_DP, NB)).astype(jnp.int32),
    }


EPSILON = 1e-06
THETA = 1000042.0
HIGHEST = lax.Precision.HIGHEST

@jax.custom_vjp
def low(v):
    return lax.optimization_barrier(v.astype(jnp.bfloat16)).astype(jnp.float32)

@jax.custom_vjp
def low_back(v):
    return v

def low_keep(v):
    return (low(v), None)

def low_pass(kept, grad):
    return (grad,)

def back_keep(v):
    return (v, None)

def back_low(kept, grad):
    return (low(grad),)
low.defvjp(low_keep, low_pass)
low_back.defvjp(back_keep, back_low)

def block_meta(counts_row, trim_row, blocks, block_width):
    number = counts_row.shape[0]
    seq_ends = jnp.cumsum(counts_row).astype(jnp.int32)
    seq_starts = (seq_ends - counts_row).astype(jnp.int32)
    limits = (counts_row * block_width - trim_row).astype(jnp.int32)
    seq_index = lax.optimization_barrier(jnp.sum((blocks[:, None] >= seq_ends[None, :]).astype(jnp.int32), axis=1)).astype(jnp.int32)
    chosen = seq_index[:, None] == jnp.arange(number, dtype=jnp.int32)[None, :]
    begin = lax.optimization_barrier(jnp.sum(jnp.where(chosen, seq_starts[None, :], 0), axis=1)).astype(jnp.int32)
    limit = lax.optimization_barrier(jnp.sum(jnp.where(chosen, limits[None, :], 0), axis=1)).astype(jnp.int32)
    offsets = jnp.arange(block_width, dtype=jnp.int32)
    position = ((blocks - begin)[:, None] * block_width + offsets[None, :]).reshape(-1).astype(jnp.int32)
    return (jnp.repeat(seq_index, block_width), position, jnp.repeat(limit, block_width), begin)

def rotary_tables(position, head_size):
    half_size = head_size // 2
    freqs = jnp.exp(jnp.arange(half_size, dtype=jnp.float32) * (-2.0 * math.log(THETA) / head_size))
    angle = position.astype(jnp.float32)[:, None] * freqs[None, :]
    return (jnp.cos(angle), jnp.sin(angle))

def rotate(values, cosine, sine):
    half_size = values.shape[-1] // 2
    first, second = (values[..., :half_size], values[..., half_size:])
    cos_wide, sin_wide = (cosine[:, None, :], sine[:, None, :])
    return jnp.concatenate([first * cos_wide - second * sin_wide, second * cos_wide + first * sin_wide], axis=-1)

def norm_rows(values):
    return values * lax.rsqrt(lax.optimization_barrier(jnp.mean(values * values, axis=1, keepdims=True)) + EPSILON)

def matmul(left, right):
    return jnp.dot(left, right, precision=HIGHEST, preferred_element_type=jnp.float32)

def matmul_t(left, right):
    return lax.dot_general(left, right, (((1,), (1,)), ((), ())), precision=HIGHEST, preferred_element_type=jnp.float32)

def group_attention(queries, keys, values, seq_tok, position, limit_tok):
    group_size = H // KVH
    keys_wide = jnp.repeat(keys, group_size, axis=1)
    values_wide = jnp.repeat(values, group_size, axis=1)
    scores = jnp.einsum('qhd,khd->hqk', queries, keys_wide, precision=HIGHEST) * HD ** (-0.5)
    scores = low_back(scores)
    allowed = (seq_tok[:, None] == seq_tok[None, :]) & (position[None, :] <= position[:, None]) & (position[None, :] < limit_tok[None, :])
    scores = jnp.where(allowed[None], scores, -1e+30)
    probs = low(jax.nn.softmax(scores, axis=-1))
    return jnp.einsum('hqk,khd->qhd', probs, values_wide, precision=HIGHEST)

def attention_all(queries, keys, values, seq_all, pos_all, lim_all):
    group_rows = NB * BLK

    def step(carry, layer_input_rows):
        return (carry, group_attention(*layer_input_rows))
    layer_input_rows = (queries.reshape(N_DP, group_rows, H, HD), keys.reshape(N_DP, group_rows, KVH, HD), values.reshape(N_DP, group_rows, KVH, HD), seq_all, pos_all, lim_all)
    _, result = lax.scan(jax.checkpoint(step), jnp.zeros((), jnp.float32), layer_input_rows)
    return result.reshape(N_DP * group_rows, H, HD)

def forward(layer_input_rows, gain_one, weight_q, weight_k, weight_v, weight_o, gain_two, weight_g, weight_u, weight_d, tables):
    cosine, sine, seq_all, pos_all, lim_all = tables
    count = layer_input_rows.shape[0]
    xn_one = low(norm_rows(layer_input_rows) * gain_one[None, :])
    q_proj = low_back(matmul(xn_one, weight_q))
    k_proj = low_back(matmul(xn_one, weight_k))
    v_proj = low_back(matmul(xn_one, weight_v))
    queries = low(rotate(q_proj.reshape(count, H, HD), cosine, sine))
    keys = low(rotate(k_proj.reshape(count, KVH, HD), cosine, sine))
    values = low(v_proj.reshape(count, KVH, HD))
    attended = attention_all(queries, keys, values, seq_all, pos_all, lim_all)
    attended = low(low_back(attended.reshape(count, H * HD)))
    branch_attn = low_back(matmul_t(attended, weight_o))
    residual_stream = layer_input_rows + branch_attn
    xn_two = low(norm_rows(residual_stream) * gain_two[None, :])
    gate = low_back(matmul(xn_two, weight_g))
    upper = low_back(matmul(xn_two, weight_u))
    hidden = low(jax.nn.silu(gate) * upper)
    branch_mlp = low_back(matmul_t(hidden, weight_d))
    return (residual_stream + branch_mlp, (branch_attn, residual_stream, branch_mlp))

def reference(tokens, cotangent, attn_norm, w_query, w_key, w_value, w_output, mlp_norm, w_gate, w_up, w_down, block_counts, trims, block_order):
    blocks = jnp.arange(NB, dtype=jnp.int32)
    seq_all, pos_all, lim_all, _ = jax.vmap(lambda counts_row, trim_row: block_meta(counts_row, trim_row, blocks, BLK))(block_counts, trims)
    position = pos_all.reshape(-1)
    valid = (pos_all < lim_all).reshape(-1).astype(jnp.float32)
    cosine, sine = rotary_tables(position, HD)
    inverse = lax.optimization_barrier(jnp.sum(jnp.where(block_order[:, :, None] == blocks[None, None, :], blocks[None, :, None], 0), axis=1)).astype(jnp.int32)
    cot_blocks = cotangent.astype(jnp.float32).reshape(N_DP, NB, BLK, D)
    cot_given = cot_blocks[jnp.arange(N_DP, dtype=jnp.int32)[:, None], inverse].reshape(-1, D) * valid[:, None]
    tables = (cosine, sine, seq_all, pos_all, lim_all)
    params = tuple((array.astype(jnp.float32) for array in (tokens, attn_norm, w_query, w_key, w_value, w_output, mlp_norm, w_gate, w_up, w_down)))
    final, pullback, extras = jax.vjp(lambda *weights: forward(*weights, tables), *params, has_aux=True)
    grads = pullback(cot_given)
    branch_attn, residual_stream, branch_mlp = extras
    count = jnp.sum(valid)
    stacked = jnp.stack([lax.optimization_barrier(jnp.sum(array * array * valid[:, None], axis=0)) for array in (branch_attn, residual_stream, branch_mlp, final)])
    rms_stats = jnp.sqrt(stacked / count)
    return (final.astype(jnp.bfloat16), grads[0].astype(jnp.bfloat16), grads[1], grads[2], grads[3], grads[4], grads[5], grads[6], grads[7], grads[8], grads[9], rms_stats)
```

```python
import functools
import math

import jax
import jax.numpy as jnp
import numpy as np
from jax import lax
from jax.experimental import pallas as pl
from jax.experimental.pallas import tpu as pltpu
from jax.sharding import Mesh
from jax.sharding import PartitionSpec as P

HD = 256
BLK = 128
EPSILON = 1e-06
THETA = 1000042.0
TP_AXES = ("zl", "y", "c")
TPN = 8
NEG = -1e30
BF = jnp.bfloat16
F32 = jnp.float32


def swap(array, axis):
    return lax.ppermute(array, axis, [(0, 1), (1, 0)])


def dot(left, right, contract, out=F32):
    got = lax.dot_general(left, right, (contract, ((), ())), preferred_element_type=F32)
    return got.astype(out)


def gather_rows(own):
    rows = own.shape[0]
    half = rows // 2
    first, second = own[:half], own[half:]
    first_y = swap(first, "y")
    second_z = swap(second, "zl")
    core_own = swap(own, "c")
    core_one = swap(jnp.stack([first_y, second_z]), "c")
    first_z = swap(jnp.stack([first, first_y]), "zl")
    second_y = swap(jnp.stack([second, second_z]), "y")
    core_two = swap(jnp.concatenate([first_z, second_y]), "c")
    pieces = [
        own,
        core_own,
        first_y,
        second_y[0],
        core_one[0],
        core_two[2],
        first_z[0],
        second_z,
        core_two[0],
        core_one[1],
        first_z[1],
        second_y[1],
        core_two[1],
        core_two[3],
    ]
    return jnp.concatenate(pieces, axis=0).reshape(TPN, rows, own.shape[1])


def scatter_sum(parts):
    rows = parts.shape[1]
    half = rows // 2
    met = swap(parts[1::2], "c").astype(F32)
    total = parts[0::2].astype(F32) + met
    first, second = total[:, :half], total[:, half:]
    low_first, low_second = first.astype(BF), second.astype(BF)
    got_first = swap(low_first[1::2], "y").astype(F32)
    got_second = swap(low_second[2:], "zl").astype(F32)
    first = first[0::2] + got_first
    second = second[:2] + got_second
    got_first = swap(first[1].astype(BF), "zl").astype(F32)
    got_second = swap(second[1].astype(BF), "y").astype(F32)
    return jnp.concatenate([first[0] + got_first, second[0] + got_second], axis=0)


def gather_weight(piece, columns, dp_axes):
    rows = piece.shape[0]
    mine = lax.all_to_all(piece, TP_AXES, 1, 0, tiled=True).reshape(rows * TPN, columns)
    for axis in ("zh",) + dp_axes[::-1]:
        other = swap(mine, axis)
        low = lax.axis_index(axis) == 0
        mine = jnp.concatenate([jnp.where(low, mine, other), jnp.where(low, other, mine)], axis=0)
    return mine


def reduce_weight(partial, dp_axes):
    mine = partial
    for axis in dp_axes + ("zh",):
        half = mine.shape[0] // 2
        place = lax.axis_index(axis)
        send = lax.dynamic_slice_in_dim(mine, (1 - place) * half, half, 0).astype(BF)
        keep = lax.dynamic_slice_in_dim(mine, place * half, half, 0)
        mine = keep.astype(F32) + swap(send, axis).astype(F32)
    rows = mine.shape[0] // TPN
    low = mine.astype(BF).reshape(TPN, rows, mine.shape[1])
    got = lax.all_to_all(low, TP_AXES, 0, 0, tiled=True)
    return jnp.swapaxes(got, 0, 1).astype(F32)


def slot_of(tile, info):
    return ((tile // TPN) ^ info[1]) * TPN + ((tile % TPN) ^ info[0])


def forward_kernel(info, q_ref, k_ref, v_ref, lo_ref, hi_ref, out_ref, lse_ref, top, total, acc):
    step = pl.program_id(0)
    rows = q_ref.shape[0]
    last = info[1] * TPN + (info[0] ^ step)
    queries = q_ref[...]
    low, high = lo_ref[...], hi_ref[...]
    top[...] = jnp.full_like(top, NEG)
    total[...] = jnp.zeros_like(total)
    acc[...] = jnp.zeros_like(acc)

    def body(tile, carry):
        start = pl.multiple_of(slot_of(tile, info) * rows, rows)
        keys = k_ref[pl.ds(start, rows), :]
        values = v_ref[pl.ds(start, rows), :]
        scores = dot(queries, keys, ((1,), (1,))) * (HD**-0.5)
        place = tile * rows + lax.broadcasted_iota(jnp.int32, scores.shape, 1)
        scores = jnp.where((place >= low) & (place <= high), scores, NEG)
        before = top[...]
        now = jnp.maximum(before, jnp.max(scores, axis=1, keepdims=True))
        prob = jnp.exp(scores - now)
        fade = jnp.exp(before - now)
        top[...] = now
        total[...] = total[...] * fade + jnp.sum(prob, axis=1, keepdims=True)
        acc[...] = acc[...] * fade + dot(prob.astype(BF), values, ((1,), (0,)))
        return carry

    lax.fori_loop(info[2 + step], last + 1, body, 0)
    out_ref[...] = (acc[...] / total[...]).astype(BF)
    lse_ref[...] = top[...] + jnp.log(total[...])


def backward_kernel(
    info, q_ref, k_ref, v_ref, lo_ref, hi_ref, lse_ref, delta_ref, grad_ref, gq_ref, gk_ref, gv_ref, acc
):
    step = pl.program_id(0)
    rows = q_ref.shape[0]
    last = info[1] * TPN + (info[0] ^ step)
    queries, grads = q_ref[...], grad_ref[...]
    low, high = lo_ref[...], hi_ref[...]
    lse, delta = lse_ref[...], delta_ref[...]
    acc[...] = jnp.zeros_like(acc)

    @pl.when(step == 0)
    def _():
        gk_ref[...] = jnp.zeros_like(gk_ref)
        gv_ref[...] = jnp.zeros_like(gv_ref)

    def body(tile, carry):
        start = pl.multiple_of(slot_of(tile, info) * rows, rows)
        keys = k_ref[pl.ds(start, rows), :]
        values = v_ref[pl.ds(start, rows), :]
        scores = dot(queries, keys, ((1,), (1,))) * (HD**-0.5)
        place = tile * rows + lax.broadcasted_iota(jnp.int32, scores.shape, 1)
        scores = jnp.where((place >= low) & (place <= high), scores, NEG)
        prob = jnp.exp(scores - lse)
        dprob = dot(grads, values, ((1,), (1,)))
        dscore = (prob * (dprob - delta)).astype(BF)
        acc[...] += dot(dscore, keys, ((1,), (0,)))
        gk_ref[pl.ds(start, rows), :] += dot(dscore, queries, ((0,), (0,))) * (HD**-0.5)
        gv_ref[pl.ds(start, rows), :] += dot(prob.astype(BF), grads, ((0,), (0,)))
        return carry

    lax.fori_loop(info[2 + step], last + 1, body, 0)
    gq_ref[...] = acc[...] * (HD**-0.5)


def tile_spec(rows, width):
    return pl.BlockSpec((rows, width), lambda i, info: (i, 0))


def whole_spec(rows, width):
    return pl.BlockSpec((rows, width), lambda i, info: (0, 0))


def attention_forward(info, queries, keys, values, low, high):
    count, rows = queries.shape[0], queries.shape[0] // TPN
    span = keys.shape[0]
    return pl.pallas_call(
        forward_kernel,
        grid_spec=pltpu.PrefetchScalarGridSpec(
            num_scalar_prefetch=1,
            grid=(TPN,),
            in_specs=[
                tile_spec(rows, HD),
                whole_spec(span, HD),
                whole_spec(span, HD),
                tile_spec(rows, 1),
                tile_spec(rows, 1),
            ],
            out_specs=[tile_spec(rows, HD), tile_spec(rows, 1)],
            scratch_shapes=[
                pltpu.VMEM((rows, 1), F32),
                pltpu.VMEM((rows, 1), F32),
                pltpu.VMEM((rows, HD), F32),
            ],
        ),
        out_shape=[
            jax.ShapeDtypeStruct((count, HD), BF),
            jax.ShapeDtypeStruct((count, 1), F32),
        ],
        compiler_params=pltpu.CompilerParams(vmem_limit_bytes=40 << 20),
        cost_estimate=pl.CostEstimate(
            flops=4 * count * count * HD, bytes_accessed=8 << 20, transcendentals=count * count
        ),
        name="attend",
    )(info, queries, keys, values, low, high)


def attention_backward(info, queries, keys, values, low, high, lse, delta, grads):
    count, rows = queries.shape[0], queries.shape[0] // TPN
    span = keys.shape[0]
    return pl.pallas_call(
        backward_kernel,
        grid_spec=pltpu.PrefetchScalarGridSpec(
            num_scalar_prefetch=1,
            grid=(TPN,),
            in_specs=[
                tile_spec(rows, HD),
                whole_spec(span, HD),
                whole_spec(span, HD),
                tile_spec(rows, 1),
                tile_spec(rows, 1),
                tile_spec(rows, 1),
                tile_spec(rows, 1),
                tile_spec(rows, HD),
            ],
            out_specs=[tile_spec(rows, HD), whole_spec(span, HD), whole_spec(span, HD)],
            scratch_shapes=[pltpu.VMEM((rows, HD), F32)],
        ),
        out_shape=[
            jax.ShapeDtypeStruct((count, HD), F32),
            jax.ShapeDtypeStruct((span, HD), F32),
            jax.ShapeDtypeStruct((span, HD), F32),
        ],
        compiler_params=pltpu.CompilerParams(vmem_limit_bytes=48 << 20),
        cost_estimate=pl.CostEstimate(
            flops=10 * count * count * HD, bytes_accessed=16 << 20, transcendentals=count * count
        ),
        name="attend_back",
    )(info, queries, keys, values, low, high, lse, delta, grads)


def pick_kernel(index, block_ref, valid_ref, out_ref):
    out_ref[...] = block_ref[...] * valid_ref[...].astype(BF)


def pick_blocks(index, blocks, valid):
    count, width = index.shape[0], blocks.shape[1]
    return pl.pallas_call(
        pick_kernel,
        grid_spec=pltpu.PrefetchScalarGridSpec(
            num_scalar_prefetch=1,
            grid=(count,),
            in_specs=[
                pl.BlockSpec((BLK, width), lambda i, index: (index[i], 0)),
                pl.BlockSpec((BLK, 1), lambda i, index: (i, 0)),
            ],
            out_specs=pl.BlockSpec((BLK, width), lambda i, index: (i, 0)),
        ),
        out_shape=jax.ShapeDtypeStruct((count * BLK, width), BF),
        cost_estimate=pl.CostEstimate(flops=0, bytes_accessed=4 * count * BLK * width, transcendentals=0),
        name="pick",
    )(index, blocks, valid)


def rms_scale(values):
    return lax.rsqrt(jnp.mean(values * values, axis=1, keepdims=True) + EPSILON)


def rotate(values, cosine, sine):
    half = HD // 2
    first, second = values[:, :half], values[:, half:]
    return jnp.concatenate([first * cosine - second * sine, second * cosine + first * sine], axis=1)


def flip_pairs(array):
    tiles = array.reshape(-1, 2, 2 * BLK, array.shape[1])
    return jnp.stack([tiles[:, 1], tiles[:, 0]], axis=1).reshape(array.shape)


def shards(
    dp_axes,
    tokens,
    cotangent,
    attn_norm,
    w_query,
    w_key,
    w_value,
    w_output,
    mlp_norm,
    w_gate,
    w_up,
    w_down,
    block_counts,
    trims,
    block_order,
):
    every = dp_axes + ("zh",) + TP_AXES
    rows, width = tokens.shape
    count = rows * TPN
    weight_rows = w_gate.shape[0]
    ff_part = w_gate.shape[1] // TPN
    rank = lax.axis_index(TP_AXES)
    upper = lax.axis_index("zh")
    core = lax.axis_index("c")
    group = lax.axis_index(dp_axes)

    counts_row = lax.dynamic_slice_in_dim(block_counts, group, 1, 0)[0]
    trim_row = lax.dynamic_slice_in_dim(trims, group, 1, 0)[0]
    order_row = lax.dynamic_slice_in_dim(block_order, group, 1, 0)[0]
    number = counts_row.shape[0]
    earlier = np.tril(np.ones((number, number), np.int32))
    seq_ends = jnp.sum(jnp.asarray(earlier) * counts_row[None, :], axis=1)
    seq_starts = seq_ends - counts_row
    ranks = rank ^ jnp.arange(TPN, dtype=jnp.int32)
    tiles = upper * TPN + ranks
    index = (tiles[:, None] * rows + jnp.arange(rows, dtype=jnp.int32)[None, :]).reshape(-1)
    block = index // BLK
    inside = (block[:, None] >= seq_starts[None, :]) & (block[:, None] < seq_ends[None, :])
    low = jnp.sum(jnp.where(inside, seq_starts[None, :] * BLK, 0), axis=1)
    limit = jnp.sum(jnp.where(inside, (counts_row * BLK - trim_row)[None, :], 0), axis=1)
    position = index - low
    valid = (position < limit).astype(F32)[:, None]
    high = jnp.minimum(index, low + limit - 1)
    info = jnp.concatenate(
        [
            jnp.stack([rank, upper]).astype(jnp.int32),
            (low.reshape(TPN, rows)[:, 0] // rows).astype(jnp.int32),
        ]
    )
    low, high = low[:, None], high[:, None]
    freqs = jnp.exp(jnp.arange(HD // 2, dtype=F32) * (-2.0 * math.log(THETA) / HD))
    angle = position.astype(F32)[:, None] * freqs[None, :]
    cosine, sine = jnp.cos(angle), jnp.sin(angle)
    is_key = core == 0
    cosine_kv = jnp.where(is_key, cosine, 1.0)
    sine_kv = jnp.where(is_key, sine, 0.0)

    def ranked(weight):
        return weight.reshape(weight_rows, TPN, -1)

    key_value = jnp.stack(
        [w_key.reshape(weight_rows, TPN // 2, HD), w_value.reshape(weight_rows, TPN // 2, HD)], axis=2
    ).reshape(weight_rows, TPN, HD)
    gains = lax.all_gather(jnp.stack([attn_norm, mlp_norm])[None], every, axis=0, tiled=True)
    gains = jnp.swapaxes(gains, 0, 1).reshape(2, 1, width).astype(F32)
    gain_one, gain_two = gains[0], gains[1]
    attn_in = gather_weight(jnp.concatenate([ranked(w_query), key_value], axis=2), 2 * HD, dp_axes)
    attn_out = gather_weight(ranked(w_output), HD, dp_axes)
    gate_up = gather_weight(jnp.concatenate([ranked(w_gate), ranked(w_up)], axis=2), 2 * ff_part, dp_axes)
    down = gather_weight(ranked(w_down), ff_part, dp_axes)

    x_all = gather_rows(tokens).reshape(count, width).astype(F32)
    xn_one = (x_all * rms_scale(x_all) * gain_one).astype(BF)
    projected = dot(xn_one, attn_in, ((1,), (0,)))
    queries = rotate(projected[:, :HD], cosine, sine).astype(BF)
    kv_mine = rotate(projected[:, HD:], cosine_kv, sine_kv).astype(BF)
    kv_lower = lax.ppermute(kv_mine, "zh", [(0, 1)])
    kv_all = jnp.concatenate([kv_mine, kv_lower], axis=0)
    kv_other = jnp.concatenate([flip_pairs(swap(kv_mine, "c")), flip_pairs(swap(kv_lower, "c"))], axis=0)
    keys = jnp.where(is_key, kv_all, kv_other)
    values = jnp.where(is_key, kv_other, kv_all)
    attended, lse = attention_forward(info, queries, keys, values, low, high)
    branch_parts = dot(attended, attn_out, ((1,), (1,)), BF)
    branch_attn = scatter_sum(branch_parts.reshape(TPN, rows, width))

    x_own = tokens.astype(F32)
    scale_one = rms_scale(x_own)
    xhat_one = x_own * scale_one
    resid = x_own + branch_attn
    scale_two = rms_scale(resid)
    xhat_two = resid * scale_two
    xn_two = gather_rows((xhat_two * gain_two).astype(BF)).reshape(count, width)

    slots = order_row.shape[0]
    per_rank = rows // BLK
    slot_ids = jnp.arange(slots, dtype=jnp.int32)
    home = (tiles[:, None] * per_rank + jnp.arange(per_rank, dtype=jnp.int32)[None, :]).reshape(-1)
    slot = jnp.sum(jnp.where(order_row[None, :] == home[:, None], slot_ids[None, :], 0), axis=1)
    owner = (slot // per_rank) ^ (upper * TPN + rank)
    pick = ((owner % TPN) * 2 + owner // TPN) * per_rank + slot % per_rank
    cot_pair = jnp.concatenate([cotangent, swap(cotangent, "zh")], axis=0)
    cot_all = gather_rows(cot_pair).reshape(-1, width)
    grad_mlp = pick_blocks(pick.astype(jnp.int32), cot_all, valid)

    gate_up_out = dot(xn_two, gate_up, ((1,), (0,)))
    gate, up = gate_up_out[:, :ff_part], gate_up_out[:, ff_part:]
    sigma = jax.nn.sigmoid(gate)
    activated = gate * sigma
    hidden = (activated * up).astype(BF)
    grad_hidden = dot(grad_mlp, down, ((1,), (0,)))
    grad_up_act = (grad_hidden * activated).astype(BF)
    grad_gate_act = (grad_hidden * up * sigma * (1.0 + gate * (1.0 - sigma))).astype(BF)
    grad_both = jnp.concatenate([grad_gate_act, grad_up_act], axis=1)
    grad_xn_two_parts = dot(grad_both, gate_up, ((1,), (1,)), BF)
    grad_xn_two = scatter_sum(grad_xn_two_parts.reshape(TPN, rows, width))
    mlp_parts = dot(hidden, down, ((1,), (1,)), BF)
    branch_mlp = scatter_sum(mlp_parts.reshape(TPN, rows, width))
    grad_gate_up_w = reduce_weight(dot(xn_two, grad_both, ((0,), (0,)), BF), dp_axes)
    grad_down_w = reduce_weight(dot(grad_mlp, hidden, ((0,), (0,)), BF), dp_axes)

    final = resid + branch_mlp
    output = final.astype(BF)
    valid_own = valid[:rows]
    squares = [jnp.sum(a * a * valid_own, axis=0) for a in (branch_attn, resid, branch_mlp, final)]

    grad_final = grad_mlp[:rows].astype(F32)
    gradient_two = jnp.sum(grad_xn_two * xhat_two, axis=0)
    scaled = grad_xn_two * gain_two
    grad_resid = grad_final + scale_two * (
        scaled - xhat_two * jnp.mean(scaled * xhat_two, axis=1, keepdims=True)
    )
    grad_branch = gather_rows(grad_resid.astype(BF)).reshape(count, width)
    grad_attn_f32 = dot(grad_branch, attn_out, ((1,), (0,)))
    grad_attn = grad_attn_f32.astype(BF)
    delta = jnp.sum(grad_attn.astype(F32) * attended.astype(F32), axis=1, keepdims=True)
    grad_q, grad_k, grad_v = attention_backward(
        info, queries, keys, values, low, high, lse, delta, grad_attn
    )
    send = jnp.where(is_key, grad_v, grad_k).astype(BF)
    keep = jnp.where(is_key, grad_k, grad_v)
    chip = keep + flip_pairs(swap(send, "c")).astype(F32)
    from_upper = lax.ppermute(chip[count:].astype(BF), "zh", [(1, 0)])
    grad_kv = chip[:count] + from_upper.astype(F32)
    grad_q_proj = rotate(grad_q, cosine, -sine).astype(BF)
    grad_kv_proj = rotate(grad_kv, cosine_kv, -sine_kv).astype(BF)
    grad_proj = jnp.concatenate([grad_q_proj, grad_kv_proj], axis=1)
    grad_xn_one_parts = dot(grad_proj, attn_in, ((1,), (1,)), BF)
    grad_xn_one = scatter_sum(grad_xn_one_parts.reshape(TPN, rows, width))
    grad_in_w = reduce_weight(dot(xn_one, grad_proj, ((0,), (0,)), BF), dp_axes)
    grad_out_w = reduce_weight(dot(grad_branch, attended, ((0,), (0,)), BF), dp_axes)

    gradient_one = jnp.sum(grad_xn_one * xhat_one, axis=0)
    scaled = grad_xn_one * gain_one
    input_grad = grad_resid + scale_one * (
        scaled - xhat_one * jnp.mean(scaled * xhat_one, axis=1, keepdims=True)
    )
    sums = jnp.stack(squares + [gradient_one, gradient_two], axis=1)
    sums = lax.psum_scatter(sums, every, scatter_dimension=0, tiled=True)
    valid_count = jnp.sum((block_counts * BLK - trims).astype(F32))
    rms_stats = jnp.sqrt(sums[:, :4] / valid_count).T

    def flat(array):
        return array.reshape(weight_rows, -1)

    grad_kv_w = grad_in_w[:, :, HD:].reshape(weight_rows, TPN // 2, 2, HD)
    return (
        output,
        input_grad.astype(BF),
        sums[:, 4],
        flat(grad_in_w[:, :, :HD]),
        flat(grad_kv_w[:, :, 0]),
        flat(grad_kv_w[:, :, 1]),
        flat(grad_out_w),
        sums[:, 5],
        flat(grad_gate_up_w[:, :, :ff_part]),
        flat(grad_gate_up_w[:, :, ff_part:]),
        flat(grad_down_w),
        rms_stats,
    )


def solution(mesh):
    outer = mesh.shape["dp"]
    bits = outer.bit_length() - 1
    dp_axes = tuple(f"x{i}" for i in range(bits))
    names = dp_axes + ("zh",) + TP_AXES
    fine = Mesh(mesh.devices.reshape((2,) * len(names)), names)
    rows, flat = P(names, None), P(names)
    in_specs = (rows, rows, flat, rows, rows, rows, rows, flat, rows, rows, rows, P(), P(), P())
    out_specs = (rows, rows, flat, rows, rows, rows, rows, flat, rows, rows, rows, P(None, names))
    return jax.shard_map(
        functools.partial(shards, dp_axes),
        mesh=fine,
        in_specs=in_specs,
        out_specs=out_specs,
        check_vma=False,
    )
```

```python
import functools
import math

import jax
import jax.numpy as jnp
import numpy as np
from jax import lax
from jax.experimental import pallas as pl
from jax.experimental.pallas import tpu as pltpu
from jax.sharding import Mesh
from jax.sharding import PartitionSpec as P

HD = 256
BLK = 128
EPSILON = 1e-06
THETA = 1000042.0
TP_AXES = ("zl", "y", "c")
TPN = 8
NEG = -1e30
BF = jnp.bfloat16
F32 = jnp.float32


def swap(array, axis):
    return lax.ppermute(array, axis, [(0, 1), (1, 0)])


def dot(left, right, contract, out=F32):
    got = lax.dot_general(left, right, (contract, ((), ())), preferred_element_type=F32)
    return got.astype(out)


def after(array, *others):
    return lax.optimization_barrier((array,) + others)[0]


def gather_rows(own):
    rows = own.shape[0]
    half = rows // 2
    first, second = own[:half], own[half:]
    first_y = swap(first, "y")
    second_z = swap(second, "zl")
    core_own = swap(own, "c")
    core_one = swap(jnp.stack([first_y, second_z]), "c")
    first_z = swap(jnp.stack([first, first_y]), "zl")
    second_y = swap(jnp.stack([second, second_z]), "y")
    core_two = swap(jnp.concatenate([first_z, second_y]), "c")
    pieces = [
        own,
        core_own,
        first_y,
        second_y[0],
        core_one[0],
        core_two[2],
        first_z[0],
        second_z,
        core_two[0],
        core_one[1],
        first_z[1],
        second_y[1],
        core_two[1],
        core_two[3],
    ]
    return jnp.concatenate(pieces, axis=0).reshape(TPN, rows, own.shape[1])


def scatter_sum(parts):
    rows = parts.shape[1]
    half = rows // 2
    met = swap(parts[1::2], "c").astype(F32)
    total = parts[0::2].astype(F32) + met
    first, second = total[:, :half], total[:, half:]
    low_first, low_second = first.astype(BF), second.astype(BF)
    got_first = swap(low_first[1::2], "y").astype(F32)
    got_second = swap(low_second[2:], "zl").astype(F32)
    first = first[0::2] + got_first
    second = second[:2] + got_second
    got_first = swap(first[1].astype(BF), "zl").astype(F32)
    got_second = swap(second[1].astype(BF), "y").astype(F32)
    return jnp.concatenate([first[0] + got_first, second[0] + got_second], axis=0)


def deal_columns(piece):
    rows, _, columns = piece.shape
    return lax.all_to_all(piece, TP_AXES, 1, 0, tiled=True).reshape(rows * TPN, columns)


def in_order(mine, other, axis):
    low = lax.axis_index(axis) == 0
    return jnp.concatenate([jnp.where(low, mine, other), jnp.where(low, other, mine)], axis=0)


def gather_outer(mine, dp_axes):
    for axis in dp_axes[::-1]:
        mine = in_order(mine, swap(mine, axis), axis)
    return mine


def halve(partial, axis):
    half = partial.shape[0] // 2
    place = lax.axis_index(axis)
    send = lax.dynamic_slice_in_dim(partial, (1 - place) * half, half, 0).astype(BF)
    keep = lax.dynamic_slice_in_dim(partial, place * half, half, 0)
    return swap(send, axis), keep


def add_up(got, keep):
    return keep.astype(F32) + got.astype(F32)


def deal_rows(mine):
    rows = mine.shape[0] // TPN
    low = mine.astype(BF).reshape(TPN, rows, mine.shape[1])
    got = lax.all_to_all(low, TP_AXES, 0, 0, tiled=True)
    return jnp.swapaxes(got, 0, 1).astype(F32)


def slot_of(tile, info):
    return ((tile // TPN) ^ info[1]) * TPN + ((tile % TPN) ^ info[0])


def forward_kernel(info, q_ref, k_ref, v_ref, lo_ref, hi_ref, out_ref, lse_ref, top, total, acc):
    step = pl.program_id(0)
    rows = q_ref.shape[0]
    last = info[1] * TPN + (info[0] ^ step)
    queries = q_ref[...]
    low, high = lo_ref[...], hi_ref[...]
    top[...] = jnp.full_like(top, NEG)
    total[...] = jnp.zeros_like(total)
    acc[...] = jnp.zeros_like(acc)

    def body(tile, carry):
        start = pl.multiple_of(slot_of(tile, info) * rows, rows)
        keys = k_ref[pl.ds(start, rows), :]
        values = v_ref[pl.ds(start, rows), :]
        scores = dot(queries, keys, ((1,), (1,))) * (HD**-0.5)
        place = tile * rows + lax.broadcasted_iota(jnp.int32, scores.shape, 1)
        scores = jnp.where((place >= low) & (place <= high), scores, NEG)
        before = top[...]
        now = jnp.maximum(before, jnp.max(scores, axis=1, keepdims=True))
        prob = jnp.exp(scores - now)
        fade = jnp.exp(before - now)
        top[...] = now
        total[...] = total[...] * fade + jnp.sum(prob, axis=1, keepdims=True)
        acc[...] = acc[...] * fade + dot(prob.astype(BF), values, ((1,), (0,)))
        return carry

    lax.fori_loop(info[2 + step], last + 1, body, 0)
    out_ref[...] = (acc[...] / total[...]).astype(BF)
    lse_ref[...] = top[...] + jnp.log(total[...])


def backward_kernel(
    info, q_ref, k_ref, v_ref, lo_ref, hi_ref, lse_ref, delta_ref, grad_ref, gq_ref, gk_ref, gv_ref, acc
):
    step = pl.program_id(0)
    rows = q_ref.shape[0]
    last = info[1] * TPN + (info[0] ^ step)
    queries, grads = q_ref[...], grad_ref[...]
    low, high = lo_ref[...], hi_ref[...]
    lse, delta = lse_ref[...], delta_ref[...]
    acc[...] = jnp.zeros_like(acc)

    @pl.when(step == 0)
    def _():
        gk_ref[...] = jnp.zeros_like(gk_ref)
        gv_ref[...] = jnp.zeros_like(gv_ref)

    def body(tile, carry):
        start = pl.multiple_of(slot_of(tile, info) * rows, rows)
        keys = k_ref[pl.ds(start, rows), :]
        values = v_ref[pl.ds(start, rows), :]
        scores = dot(queries, keys, ((1,), (1,))) * (HD**-0.5)
        place = tile * rows + lax.broadcasted_iota(jnp.int32, scores.shape, 1)
        scores = jnp.where((place >= low) & (place <= high), scores, NEG)
        prob = jnp.exp(scores - lse)
        dprob = dot(grads, values, ((1,), (1,)))
        dscore = (prob * (dprob - delta)).astype(BF)
        acc[...] += dot(dscore, keys, ((1,), (0,)))
        gk_ref[pl.ds(start, rows), :] += dot(dscore, queries, ((0,), (0,))) * (HD**-0.5)
        gv_ref[pl.ds(start, rows), :] += dot(prob.astype(BF), grads, ((0,), (0,)))
        return carry

    lax.fori_loop(info[2 + step], last + 1, body, 0)
    gq_ref[...] = acc[...] * (HD**-0.5)


def tile_spec(rows, width):
    return pl.BlockSpec((rows, width), lambda i, info: (i, 0))


def whole_spec(rows, width):
    return pl.BlockSpec((rows, width), lambda i, info: (0, 0))


def attention_forward(info, queries, keys, values, low, high):
    count, rows = queries.shape[0], queries.shape[0] // TPN
    span = keys.shape[0]
    return pl.pallas_call(
        forward_kernel,
        grid_spec=pltpu.PrefetchScalarGridSpec(
            num_scalar_prefetch=1,
            grid=(TPN,),
            in_specs=[
                tile_spec(rows, HD),
                whole_spec(span, HD),
                whole_spec(span, HD),
                tile_spec(rows, 1),
                tile_spec(rows, 1),
            ],
            out_specs=[tile_spec(rows, HD), tile_spec(rows, 1)],
            scratch_shapes=[
                pltpu.VMEM((rows, 1), F32),
                pltpu.VMEM((rows, 1), F32),
                pltpu.VMEM((rows, HD), F32),
            ],
        ),
        out_shape=[
            jax.ShapeDtypeStruct((count, HD), BF),
            jax.ShapeDtypeStruct((count, 1), F32),
        ],
        compiler_params=pltpu.CompilerParams(vmem_limit_bytes=40 << 20),
        cost_estimate=pl.CostEstimate(
            flops=4 * count * count * HD, bytes_accessed=8 << 20, transcendentals=count * count
        ),
        name="attend",
    )(info, queries, keys, values, low, high)


def attention_backward(info, queries, keys, values, low, high, lse, delta, grads):
    count, rows = queries.shape[0], queries.shape[0] // TPN
    span = keys.shape[0]
    return pl.pallas_call(
        backward_kernel,
        grid_spec=pltpu.PrefetchScalarGridSpec(
            num_scalar_prefetch=1,
            grid=(TPN,),
            in_specs=[
                tile_spec(rows, HD),
                whole_spec(span, HD),
                whole_spec(span, HD),
                tile_spec(rows, 1),
                tile_spec(rows, 1),
                tile_spec(rows, 1),
                tile_spec(rows, 1),
                tile_spec(rows, HD),
            ],
            out_specs=[tile_spec(rows, HD), whole_spec(span, HD), whole_spec(span, HD)],
            scratch_shapes=[pltpu.VMEM((rows, HD), F32)],
        ),
        out_shape=[
            jax.ShapeDtypeStruct((count, HD), F32),
            jax.ShapeDtypeStruct((span, HD), F32),
            jax.ShapeDtypeStruct((span, HD), F32),
        ],
        compiler_params=pltpu.CompilerParams(vmem_limit_bytes=48 << 20),
        cost_estimate=pl.CostEstimate(
            flops=10 * count * count * HD, bytes_accessed=16 << 20, transcendentals=count * count
        ),
        name="attend_back",
    )(info, queries, keys, values, low, high, lse, delta, grads)


def pick_kernel(index, block_ref, valid_ref, out_ref):
    out_ref[...] = block_ref[...] * valid_ref[...].astype(BF)


def pick_blocks(index, blocks, valid):
    count, width = index.shape[0], blocks.shape[1]
    return pl.pallas_call(
        pick_kernel,
        grid_spec=pltpu.PrefetchScalarGridSpec(
            num_scalar_prefetch=1,
            grid=(count,),
            in_specs=[
                pl.BlockSpec((BLK, width), lambda i, index: (index[i], 0)),
                pl.BlockSpec((BLK, 1), lambda i, index: (i, 0)),
            ],
            out_specs=pl.BlockSpec((BLK, width), lambda i, index: (i, 0)),
        ),
        out_shape=jax.ShapeDtypeStruct((count * BLK, width), BF),
        cost_estimate=pl.CostEstimate(flops=0, bytes_accessed=4 * count * BLK * width, transcendentals=0),
        name="pick",
    )(index, blocks, valid)


def rms_scale(values):
    return lax.rsqrt(jnp.mean(values * values, axis=1, keepdims=True) + EPSILON)


def rotate(values, cosine, sine):
    half = HD // 2
    first, second = values[:, :half], values[:, half:]
    return jnp.concatenate([first * cosine - second * sine, second * cosine + first * sine], axis=1)


def flip_pairs(array):
    tiles = array.reshape(-1, 2, 2 * BLK, array.shape[1])
    return jnp.stack([tiles[:, 1], tiles[:, 0]], axis=1).reshape(array.shape)


def shards(
    dp_axes,
    tokens,
    cotangent,
    attn_norm,
    w_query,
    w_key,
    w_value,
    w_output,
    mlp_norm,
    w_gate,
    w_up,
    w_down,
    block_counts,
    trims,
    block_order,
):
    every = dp_axes + ("zh",) + TP_AXES
    rows, width = tokens.shape
    count = rows * TPN
    weight_rows = w_gate.shape[0]
    rank = lax.axis_index(TP_AXES)
    upper = lax.axis_index("zh")
    core = lax.axis_index("c")
    group = lax.axis_index(dp_axes)

    counts_row = lax.dynamic_slice_in_dim(block_counts, group, 1, 0)[0]
    trim_row = lax.dynamic_slice_in_dim(trims, group, 1, 0)[0]
    order_row = lax.dynamic_slice_in_dim(block_order, group, 1, 0)[0]
    number = counts_row.shape[0]
    earlier = np.tril(np.ones((number, number), np.int32))
    seq_ends = jnp.sum(jnp.asarray(earlier) * counts_row[None, :], axis=1)
    seq_starts = seq_ends - counts_row
    ranks = rank ^ jnp.arange(TPN, dtype=jnp.int32)
    tiles = upper * TPN + ranks
    index = (tiles[:, None] * rows + jnp.arange(rows, dtype=jnp.int32)[None, :]).reshape(-1)
    block = index // BLK
    inside = (block[:, None] >= seq_starts[None, :]) & (block[:, None] < seq_ends[None, :])
    low = jnp.sum(jnp.where(inside, seq_starts[None, :] * BLK, 0), axis=1)
    limit = jnp.sum(jnp.where(inside, (counts_row * BLK - trim_row)[None, :], 0), axis=1)
    position = index - low
    valid = (position < limit).astype(F32)[:, None]
    high = jnp.minimum(index, low + limit - 1)
    info = jnp.concatenate(
        [
            jnp.stack([rank, upper]).astype(jnp.int32),
            (low.reshape(TPN, rows)[:, 0] // rows).astype(jnp.int32),
        ]
    )
    low, high = low[:, None], high[:, None]
    freqs = jnp.exp(jnp.arange(HD // 2, dtype=F32) * (-2.0 * math.log(THETA) / HD))
    angle = position.astype(F32)[:, None] * freqs[None, :]
    cosine, sine = jnp.cos(angle), jnp.sin(angle)
    is_key = core == 0
    cosine_kv = jnp.where(is_key, cosine, 1.0)
    sine_kv = jnp.where(is_key, sine, 0.0)

    def ranked(weight):
        return weight.reshape(weight_rows, TPN, -1)

    def scaled_by(weight, gain):
        return (weight.astype(F32) * gain.astype(F32)[:, None, None]).astype(BF)

    key_value = jnp.stack(
        [w_key.reshape(weight_rows, TPN // 2, HD), w_value.reshape(weight_rows, TPN // 2, HD)], axis=2
    ).reshape(weight_rows, TPN, HD)
    attn_rows = jnp.concatenate([ranked(w_query), key_value], axis=2)
    in_part = deal_columns(scaled_by(attn_rows, attn_norm))
    in_other = swap(in_part, "zh")
    attn_in = gather_outer(in_order(in_part, in_other, "zh"), dp_axes)
    out_part = deal_columns(after(ranked(w_output), in_part))
    out_other = swap(out_part, "zh")
    attn_out = gather_outer(in_order(out_part, out_other, "zh"), dp_axes)

    slots = order_row.shape[0]
    per_rank = rows // BLK
    slot_ids = jnp.arange(slots, dtype=jnp.int32)
    home = (tiles[:, None] * per_rank + jnp.arange(per_rank, dtype=jnp.int32)[None, :]).reshape(-1)
    slot = jnp.sum(jnp.where(order_row[None, :] == home[:, None], slot_ids[None, :], 0), axis=1)
    owner = (slot // per_rank) ^ (upper * TPN + rank)
    pick = ((owner % TPN) * 2 + owner // TPN) * per_rank + slot % per_rank
    cot_mine = after(cotangent, out_other)
    cot_other = swap(cot_mine, "zh")
    cot_pair = jnp.concatenate([cot_mine, cot_other], axis=0)
    cot_all = gather_rows(cot_pair).reshape(-1, width)
    grad_mlp = pick_blocks(pick.astype(jnp.int32), cot_all, valid)

    gate_part = deal_columns(after(scaled_by(ranked(w_gate), mlp_norm), out_part))
    gate_other = swap(after(gate_part, cot_other), "zh")
    gate_w = gather_outer(in_order(gate_part, gate_other, "zh"), dp_axes)
    up_part = deal_columns(after(scaled_by(ranked(w_up), mlp_norm), gate_part))
    up_other = swap(after(up_part, gate_other), "zh")
    up_w = gather_outer(in_order(up_part, up_other, "zh"), dp_axes)
    down_part = deal_columns(after(ranked(w_down), up_part))
    down_other = swap(after(down_part, up_other), "zh")
    down = gather_outer(in_order(down_part, down_other, "zh"), dp_axes)

    x_all = gather_rows(tokens).reshape(count, width).astype(F32)
    xn_one = (x_all * rms_scale(x_all)).astype(BF)
    projected = dot(xn_one, attn_in, ((1,), (0,)))
    queries = rotate(projected[:, :HD], cosine, sine).astype(BF)
    kv_mine = rotate(projected[:, HD:], cosine_kv, sine_kv).astype(BF)
    kv_lower = lax.ppermute(kv_mine, "zh", [(0, 1)])
    kv_all = jnp.concatenate([kv_mine, kv_lower], axis=0)
    kv_other = jnp.concatenate([flip_pairs(swap(kv_mine, "c")), flip_pairs(swap(kv_lower, "c"))], axis=0)
    keys = jnp.where(is_key, kv_all, kv_other)
    values = jnp.where(is_key, kv_other, kv_all)
    attended, lse = attention_forward(info, queries, keys, values, low, high)
    branch_parts = dot(attended, attn_out, ((1,), (1,)), BF)
    branch_attn = scatter_sum(branch_parts.reshape(TPN, rows, width))

    x_own = tokens.astype(F32)
    scale_one = rms_scale(x_own)
    xhat_one = x_own * scale_one
    resid = x_own + branch_attn
    scale_two = rms_scale(resid)
    xhat_two = resid * scale_two
    xn_two = gather_rows(xhat_two.astype(BF)).reshape(count, width)

    gate = dot(xn_two, gate_w, ((1,), (0,)))
    up = dot(xn_two, up_w, ((1,), (0,)))
    sigma = jax.nn.sigmoid(gate)
    activated = gate * sigma
    hidden = (activated * up).astype(BF)
    grad_hidden = dot(grad_mlp, down, ((1,), (0,)))
    grad_up_act = (grad_hidden * activated).astype(BF)
    grad_gate_act = (grad_hidden * up * sigma * (1.0 + gate * (1.0 - sigma))).astype(BF)
    scaled_parts = dot(grad_gate_act, gate_w, ((1,), (1,))) + dot(grad_up_act, up_w, ((1,), (1,)))
    scaled_parts = scaled_parts.astype(BF)
    scaled = scatter_sum(scaled_parts.reshape(TPN, rows, width))
    outer = dp_axes[0]
    xn_late, hidden_late = after(xn_two, scaled_parts), after(hidden, scaled_parts)
    mlp_parts = dot(hidden_late, down, ((1,), (1,)), BF)
    branch_mlp = scatter_sum(mlp_parts.reshape(TPN, rows, width))
    down_got, down_keep = halve(dot(grad_mlp, hidden_late, ((0,), (0,)), BF), outer)
    gate_got, gate_keep = halve(dot(xn_late, grad_gate_act, ((0,), (0,)), BF), outer)
    up_got, up_keep = halve(dot(xn_late, grad_up_act, ((0,), (0,)), BF), outer)

    final = resid + branch_mlp
    output = final.astype(BF)
    valid_own = valid[:rows]
    squares = [jnp.sum(a * a * valid_own, axis=0) for a in (branch_attn, resid, branch_mlp, final)]

    grad_final = grad_mlp[:rows].astype(F32)
    grad_resid = grad_final + scale_two * (
        scaled - xhat_two * jnp.mean(scaled * xhat_two, axis=1, keepdims=True)
    )
    scaled_low = grad_resid.astype(BF)
    grad_branch = gather_rows(scaled_low).reshape(count, width)
    grad_attn_f32 = dot(grad_branch, attn_out, ((1,), (0,)))
    grad_attn = grad_attn_f32.astype(BF)
    delta = jnp.sum(grad_attn.astype(F32) * attended.astype(F32), axis=1, keepdims=True)
    grad_q, grad_k, grad_v = attention_backward(
        info, queries, keys, values, low, high, lse, delta, grad_attn
    )
    send = jnp.where(is_key, grad_v, grad_k).astype(BF)
    keep = jnp.where(is_key, grad_k, grad_v)
    chip = keep + flip_pairs(swap(send, "c")).astype(F32)
    from_upper = lax.ppermute(chip[count:].astype(BF), "zh", [(1, 0)])
    grad_kv = chip[:count] + from_upper.astype(F32)
    grad_q_proj = rotate(grad_q, cosine, -sine).astype(BF)
    grad_kv_proj = rotate(grad_kv, cosine_kv, -sine_kv).astype(BF)
    grad_proj = jnp.concatenate([grad_q_proj, grad_kv_proj], axis=1)
    grad_xn_one_parts = dot(grad_proj, attn_in, ((1,), (1,)), BF)
    scaled = scatter_sum(grad_xn_one_parts.reshape(TPN, rows, width))
    input_grad = grad_resid + scale_one * (
        scaled - xhat_one * jnp.mean(scaled * xhat_one, axis=1, keepdims=True)
    )

    def rest(got, keep, *others):
        mine = add_up(after(got, *others), keep)
        for axis in dp_axes[1:]:
            mine = add_up(*halve(mine, axis))
        return halve(mine, "zh")

    down_got, down_keep = rest(down_got, down_keep, scaled_low)
    out_got, out_keep = halve(dot(grad_branch, attended, ((0,), (0,)), BF), outer)
    out_got, out_keep = rest(out_got, out_keep, grad_q)
    grad_down_w = deal_rows(add_up(after(down_got, grad_q), down_keep))
    gate_got, gate_keep = rest(gate_got, gate_keep, from_upper)
    up_got, up_keep = rest(up_got, up_keep, from_upper)
    in_got, in_keep = halve(dot(xn_one, grad_proj, ((0,), (0,)), BF), outer)
    grad_out_w = deal_rows(add_up(out_got, out_keep))
    grad_gate_w = deal_rows(add_up(after(gate_got, grad_xn_one_parts), gate_keep))
    in_got, in_keep = rest(in_got, in_keep, grad_xn_one_parts)
    grad_up_w = deal_rows(add_up(after(up_got, grad_xn_one_parts), up_keep))
    grad_in_w = deal_rows(add_up(in_got, in_keep))

    def gain_gradient(*pairs):
        return sum(jnp.sum(ranked(w).astype(F32) * g, axis=(1, 2)) for w, g in pairs)

    grad_attn_norm = gain_gradient((attn_rows, grad_in_w))
    grad_mlp_norm = gain_gradient((w_gate, grad_gate_w), (w_up, grad_up_w))
    gain_one, gain_two = (g.astype(F32)[:, None, None] for g in (attn_norm, mlp_norm))
    grad_in_w, grad_gate_w, grad_up_w = grad_in_w * gain_one, grad_gate_w * gain_two, grad_up_w * gain_two

    owners = lax.axis_size(every)
    sums = jnp.swapaxes(jnp.stack(squares).reshape(4, owners, width // owners), 0, 1)
    sums = after(sums, grad_branch)
    for axis in every:
        half = sums.shape[0] // 2
        place = lax.axis_index(axis)
        send = lax.dynamic_slice_in_dim(sums, (1 - place) * half, half, 0)
        keep = lax.dynamic_slice_in_dim(sums, place * half, half, 0)
        sums = keep + swap(send, axis)
    valid_count = jnp.sum((block_counts * BLK - trims).astype(F32))
    rms_stats = jnp.sqrt(sums[0] / valid_count)

    def flat(array):
        return array.reshape(weight_rows, -1)

    grad_kv_w = grad_in_w[:, :, HD:].reshape(weight_rows, TPN // 2, 2, HD)
    return (
        output,
        input_grad.astype(BF),
        grad_attn_norm,
        flat(grad_in_w[:, :, :HD]),
        flat(grad_kv_w[:, :, 0]),
        flat(grad_kv_w[:, :, 1]),
        flat(grad_out_w),
        grad_mlp_norm,
        flat(grad_gate_w),
        flat(grad_up_w),
        flat(grad_down_w),
        rms_stats,
    )


def solution(mesh):
    outer = mesh.shape["dp"]
    bits = outer.bit_length() - 1
    dp_axes = tuple(f"x{i}" for i in range(bits))
    names = dp_axes + ("zh",) + TP_AXES
    fine = Mesh(mesh.devices.reshape((2,) * len(names)), names)
    rows, flat = P(names, None), P(names)
    in_specs = (rows, rows, flat, rows, rows, rows, rows, flat, rows, rows, rows, P(), P(), P())
    out_specs = (rows, rows, flat, rows, rows, rows, rows, flat, rows, rows, rows, P(None, names))
    return jax.shard_map(
        functools.partial(shards, dp_axes),
        mesh=fine,
        in_specs=in_specs,
        out_specs=out_specs,
        check_vma=False,
    )
```

```python
import functools
import math

import jax
import jax.numpy as jnp
import numpy as np
from jax import lax
from jax.experimental import pallas as pl
from jax.experimental.pallas import tpu as pltpu
from jax.sharding import Mesh
from jax.sharding import PartitionSpec as P

HD = 256
BLK = 128
EPSILON = 1e-06
THETA = 1000042.0
TP_AXES = ("zl", "y", "c")
TPN = 8
NEG = -1e30
BF = jnp.bfloat16
F32 = jnp.float32


def swap(array, axis):
    return lax.ppermute(array, axis, [(0, 1), (1, 0)])


def dot(left, right, contract, out=F32):
    got = lax.dot_general(left, right, (contract, ((), ())), preferred_element_type=F32)
    return got.astype(out)


def meet(*arrays):
    return lax.optimization_barrier(arrays)


def gather_rows(own, *others):
    rows = own.shape[0]
    half = rows // 2
    first, second = own[:half], own[half:]
    first_y = swap(first, "y")
    second_z = swap(second, "zl")
    core_own = swap(own, "c")
    if others:
        first_y, second_z, *others = meet(first_y, second_z, *others)
    core_one = swap(jnp.stack([first_y, second_z]), "c")
    first_z = swap(jnp.stack([first, first_y]), "zl")
    second_y = swap(jnp.stack([second, second_z]), "y")
    core_two = swap(jnp.concatenate([first_z, second_y]), "c")
    pieces = [
        own,
        core_own,
        first_y,
        second_y[0],
        core_one[0],
        core_two[2],
        first_z[0],
        second_z,
        core_two[0],
        core_one[1],
        first_z[1],
        second_y[1],
        core_two[1],
        core_two[3],
    ]
    whole = jnp.concatenate(pieces, axis=0).reshape(TPN * rows, own.shape[1])
    return (whole, *others)


def scatter_sum(parts, *others):
    parts = parts.reshape(TPN, -1, parts.shape[1])
    rows = parts.shape[1]
    half = rows // 2
    met = swap(parts[1::2], "c").astype(F32)
    total = parts[0::2].astype(F32) + met
    first, second = total[:, :half], total[:, half:]
    low_first, low_second = first.astype(BF), second.astype(BF)
    got_first = swap(low_first[1::2], "y").astype(F32)
    got_second = swap(low_second[2:], "zl").astype(F32)
    first = first[0::2] + got_first
    second = second[:2] + got_second
    last_first, last_second = first[1].astype(BF), second[1].astype(BF)
    if others:
        last_first, last_second, *others = meet(last_first, last_second, *others)
    got_first = swap(last_first, "zl").astype(F32)
    got_second = swap(last_second, "y").astype(F32)
    return (jnp.concatenate([first[0] + got_first, second[0] + got_second], axis=0), *others)


def deal_columns(piece):
    rows, _, columns = piece.shape
    return lax.all_to_all(piece, TP_AXES, 1, 0, tiled=True).reshape(rows * TPN, columns)


def in_order(mine, other, axis):
    low = lax.axis_index(axis) == 0
    return jnp.concatenate([jnp.where(low, mine, other), jnp.where(low, other, mine)], axis=0)


def gather_some(mine, axes):
    for axis in axes[:0:-1]:
        mine = in_order(mine, swap(mine, axis), axis)
    return mine, swap(mine, axes[0])


def halve(partial, axis):
    half = partial.shape[0] // 2
    place = lax.axis_index(axis)
    send = lax.dynamic_slice_in_dim(partial, (1 - place) * half, half, 0).astype(BF)
    keep = lax.dynamic_slice_in_dim(partial, place * half, half, 0)
    return swap(send, axis), keep


def add_up(got, keep):
    return keep.astype(F32) + got.astype(F32)


def deal_rows(mine):
    rows = mine.shape[0] // TPN
    low = mine.astype(BF).reshape(TPN, rows, mine.shape[1])
    got = lax.all_to_all(low, TP_AXES, 0, 0, tiled=True)
    return jnp.swapaxes(got, 0, 1).astype(F32)


def slot_of(tile, info):
    return ((tile // TPN) ^ info[1]) * TPN + ((tile % TPN) ^ info[0])


def forward_kernel(info, q_ref, k_ref, v_ref, lo_ref, hi_ref, out_ref, lse_ref, top, total, acc):
    step = pl.program_id(0)
    rows = q_ref.shape[0]
    last = info[1] * TPN + (info[0] ^ step)
    queries = q_ref[...]
    low, high = lo_ref[...], hi_ref[...]
    top[...] = jnp.full_like(top, NEG)
    total[...] = jnp.zeros_like(total)
    acc[...] = jnp.zeros_like(acc)

    def body(tile, carry):
        start = pl.multiple_of(slot_of(tile, info) * rows, rows)
        keys = k_ref[pl.ds(start, rows), :]
        values = v_ref[pl.ds(start, rows), :]
        scores = dot(queries, keys, ((1,), (1,))) * (HD**-0.5)
        place = tile * rows + lax.broadcasted_iota(jnp.int32, scores.shape, 1)
        scores = jnp.where((place >= low) & (place <= high), scores, NEG)
        before = top[...]
        now = jnp.maximum(before, jnp.max(scores, axis=1, keepdims=True))
        prob = jnp.exp(scores - now)
        fade = jnp.exp(before - now)
        top[...] = now
        total[...] = total[...] * fade + jnp.sum(prob, axis=1, keepdims=True)
        acc[...] = acc[...] * fade + dot(prob.astype(BF), values, ((1,), (0,)))
        return carry

    lax.fori_loop(info[2 + step], last + 1, body, 0)
    out_ref[...] = (acc[...] / total[...]).astype(BF)
    lse_ref[...] = top[...] + jnp.log(total[...])


def backward_kernel(
    info, q_ref, k_ref, v_ref, lo_ref, hi_ref, lse_ref, delta_ref, grad_ref, gq_ref, gk_ref, gv_ref, acc
):
    step = pl.program_id(0)
    rows = q_ref.shape[0]
    last = info[1] * TPN + (info[0] ^ step)
    queries, grads = q_ref[...], grad_ref[...]
    low, high = lo_ref[...], hi_ref[...]
    lse, delta = lse_ref[...], delta_ref[...]
    acc[...] = jnp.zeros_like(acc)

    @pl.when(step == 0)
    def _():
        gk_ref[...] = jnp.zeros_like(gk_ref)
        gv_ref[...] = jnp.zeros_like(gv_ref)

    def body(tile, carry):
        start = pl.multiple_of(slot_of(tile, info) * rows, rows)
        keys = k_ref[pl.ds(start, rows), :]
        values = v_ref[pl.ds(start, rows), :]
        scores = dot(queries, keys, ((1,), (1,))) * (HD**-0.5)
        place = tile * rows + lax.broadcasted_iota(jnp.int32, scores.shape, 1)
        scores = jnp.where((place >= low) & (place <= high), scores, NEG)
        prob = jnp.exp(scores - lse)
        dprob = dot(grads, values, ((1,), (1,)))
        dscore = (prob * (dprob - delta)).astype(BF)
        acc[...] += dot(dscore, keys, ((1,), (0,)))
        gk_ref[pl.ds(start, rows), :] += dot(dscore, queries, ((0,), (0,))) * (HD**-0.5)
        gv_ref[pl.ds(start, rows), :] += dot(prob.astype(BF), grads, ((0,), (0,)))
        return carry

    lax.fori_loop(info[2 + step], last + 1, body, 0)
    gq_ref[...] = acc[...] * (HD**-0.5)


def tile_spec(rows, width):
    return pl.BlockSpec((rows, width), lambda i, info: (i, 0))


def whole_spec(rows, width):
    return pl.BlockSpec((rows, width), lambda i, info: (0, 0))


def attention_forward(info, queries, keys, values, low, high):
    count, rows = queries.shape[0], queries.shape[0] // TPN
    span = keys.shape[0]
    return pl.pallas_call(
        forward_kernel,
        grid_spec=pltpu.PrefetchScalarGridSpec(
            num_scalar_prefetch=1,
            grid=(TPN,),
            in_specs=[
                tile_spec(rows, HD),
                whole_spec(span, HD),
                whole_spec(span, HD),
                tile_spec(rows, 1),
                tile_spec(rows, 1),
            ],
            out_specs=[tile_spec(rows, HD), tile_spec(rows, 1)],
            scratch_shapes=[
                pltpu.VMEM((rows, 1), F32),
                pltpu.VMEM((rows, 1), F32),
                pltpu.VMEM((rows, HD), F32),
            ],
        ),
        out_shape=[
            jax.ShapeDtypeStruct((count, HD), BF),
            jax.ShapeDtypeStruct((count, 1), F32),
        ],
        compiler_params=pltpu.CompilerParams(vmem_limit_bytes=40 << 20),
        cost_estimate=pl.CostEstimate(
            flops=4 * count * count * HD, bytes_accessed=8 << 20, transcendentals=count * count
        ),
        name="attend",
    )(info, queries, keys, values, low, high)


def attention_backward(info, queries, keys, values, low, high, lse, delta, grads):
    count, rows = queries.shape[0], queries.shape[0] // TPN
    span = keys.shape[0]
    return pl.pallas_call(
        backward_kernel,
        grid_spec=pltpu.PrefetchScalarGridSpec(
            num_scalar_prefetch=1,
            grid=(TPN,),
            in_specs=[
                tile_spec(rows, HD),
                whole_spec(span, HD),
                whole_spec(span, HD),
                tile_spec(rows, 1),
                tile_spec(rows, 1),
                tile_spec(rows, 1),
                tile_spec(rows, 1),
                tile_spec(rows, HD),
            ],
            out_specs=[tile_spec(rows, HD), whole_spec(span, HD), whole_spec(span, HD)],
            scratch_shapes=[pltpu.VMEM((rows, HD), F32)],
        ),
        out_shape=[
            jax.ShapeDtypeStruct((count, HD), F32),
            jax.ShapeDtypeStruct((span, HD), F32),
            jax.ShapeDtypeStruct((span, HD), F32),
        ],
        compiler_params=pltpu.CompilerParams(vmem_limit_bytes=48 << 20),
        cost_estimate=pl.CostEstimate(
            flops=10 * count * count * HD, bytes_accessed=16 << 20, transcendentals=count * count
        ),
        name="attend_back",
    )(info, queries, keys, values, low, high, lse, delta, grads)


def pick_kernel(index, block_ref, valid_ref, out_ref):
    out_ref[...] = block_ref[...] * valid_ref[...].astype(BF)


def pick_blocks(index, blocks, valid):
    count, width = index.shape[0], blocks.shape[1]
    return pl.pallas_call(
        pick_kernel,
        grid_spec=pltpu.PrefetchScalarGridSpec(
            num_scalar_prefetch=1,
            grid=(count,),
            in_specs=[
                pl.BlockSpec((BLK, width), lambda i, index: (index[i], 0)),
                pl.BlockSpec((BLK, 1), lambda i, index: (i, 0)),
            ],
            out_specs=pl.BlockSpec((BLK, width), lambda i, index: (i, 0)),
        ),
        out_shape=jax.ShapeDtypeStruct((count * BLK, width), BF),
        cost_estimate=pl.CostEstimate(flops=0, bytes_accessed=4 * count * BLK * width, transcendentals=0),
        name="pick",
    )(index, blocks, valid)


def rms_scale(values):
    return lax.rsqrt(jnp.mean(values * values, axis=1, keepdims=True) + EPSILON)


def rotate(values, cosine, sine):
    half = HD // 2
    first, second = values[:, :half], values[:, half:]
    return jnp.concatenate([first * cosine - second * sine, second * cosine + first * sine], axis=1)


def flip_pairs(array):
    tiles = array.reshape(-1, 2, 2 * BLK, array.shape[1])
    return jnp.stack([tiles[:, 1], tiles[:, 0]], axis=1).reshape(array.shape)


def shards(
    dp_axes,
    tokens,
    cotangent,
    attn_norm,
    w_query,
    w_key,
    w_value,
    w_output,
    mlp_norm,
    w_gate,
    w_up,
    w_down,
    block_counts,
    trims,
    block_order,
):
    rows, width = tokens.shape
    count = rows * TPN
    weight_rows = w_gate.shape[0]
    rank = lax.axis_index(TP_AXES)
    upper = lax.axis_index("zh")
    core = lax.axis_index("c")
    group = lax.axis_index(dp_axes)

    counts_row = lax.dynamic_slice_in_dim(block_counts, group, 1, 0)[0]
    trim_row = lax.dynamic_slice_in_dim(trims, group, 1, 0)[0]
    order_row = lax.dynamic_slice_in_dim(block_order, group, 1, 0)[0]
    number = counts_row.shape[0]
    earlier = np.tril(np.ones((number, number), np.int32))
    seq_ends = jnp.sum(jnp.asarray(earlier) * counts_row[None, :], axis=1)
    seq_starts = seq_ends - counts_row
    ranks = rank ^ jnp.arange(TPN, dtype=jnp.int32)
    tiles = upper * TPN + ranks
    index = (tiles[:, None] * rows + jnp.arange(rows, dtype=jnp.int32)[None, :]).reshape(-1)
    block = index // BLK
    inside = (block[:, None] >= seq_starts[None, :]) & (block[:, None] < seq_ends[None, :])
    low = jnp.sum(jnp.where(inside, seq_starts[None, :] * BLK, 0), axis=1)
    limit = jnp.sum(jnp.where(inside, (counts_row * BLK - trim_row)[None, :], 0), axis=1)
    position = index - low
    valid = (position < limit).astype(F32)[:, None]
    high = jnp.minimum(index, low + limit - 1)
    info = jnp.concatenate(
        [
            jnp.stack([rank, upper]).astype(jnp.int32),
            (low.reshape(TPN, rows)[:, 0] // rows).astype(jnp.int32),
        ]
    )
    low, high = low[:, None], high[:, None]
    freqs = jnp.exp(jnp.arange(HD // 2, dtype=F32) * (-2.0 * math.log(THETA) / HD))
    angle = position.astype(F32)[:, None] * freqs[None, :]
    cosine, sine = jnp.cos(angle), jnp.sin(angle)
    is_key = core == 0
    cosine_kv = jnp.where(is_key, cosine, 1.0)
    sine_kv = jnp.where(is_key, sine, 0.0)

    def ranked(weight):
        return weight.reshape(weight_rows, TPN, -1)

    def scaled_by(weight, gain):
        return (weight.astype(F32) * gain.astype(F32)[:, None, None]).astype(BF)

    key_value = jnp.stack(
        [w_key.reshape(weight_rows, TPN // 2, HD), w_value.reshape(weight_rows, TPN // 2, HD)], axis=2
    ).reshape(weight_rows, TPN, HD)
    attn_rows = jnp.concatenate([ranked(w_query), key_value], axis=2)
    in_part = deal_columns(scaled_by(attn_rows, attn_norm))
    slots = order_row.shape[0]
    per_rank = rows // BLK
    slot_ids = jnp.arange(slots, dtype=jnp.int32)
    home = (tiles[:, None] * per_rank + jnp.arange(per_rank, dtype=jnp.int32)[None, :]).reshape(-1)
    slot = jnp.sum(jnp.where(order_row[None, :] == home[:, None], slot_ids[None, :], 0), axis=1)

    def outer_gather(part, other):
        return gather_some(in_order(part, other, "zh"), dp_axes)

    x_low, in_part = gather_rows(tokens, in_part)
    in_mine, in_other = outer_gather(in_part, swap(in_part, "zh"))
    attn_in = in_order(in_mine, in_other, dp_axes[0])
    x_all = x_low.astype(F32)
    xn_one = (x_all * rms_scale(x_all)).astype(BF)
    fsdp = dp_axes + ("zh",)
    w_output, w_gate_late, w_up_late, w_down_late, in_part = meet(w_output, w_gate, w_up, w_down, in_part)
    out_part = deal_columns(ranked(w_output))
    attn_out = lax.all_gather(out_part, fsdp, axis=0, tiled=True)
    gate_part = deal_columns(scaled_by(ranked(w_gate_late), mlp_norm))
    gate_w = lax.all_gather(gate_part, fsdp, axis=0, tiled=True)
    up_part = deal_columns(scaled_by(ranked(w_up_late), mlp_norm))
    up_w = lax.all_gather(up_part, fsdp, axis=0, tiled=True)
    down_part = deal_columns(ranked(w_down_late))
    down = lax.all_gather(down_part, fsdp, axis=0, tiled=True)
    cot_all = lax.all_gather(cotangent, ("zh",) + TP_AXES, axis=0, tiled=True)
    projected = dot(xn_one, attn_in, ((1,), (0,)))
    queries = rotate(projected[:, :HD], cosine, sine).astype(BF)
    kv_mine = rotate(projected[:, HD:], cosine_kv, sine_kv).astype(BF)
    kv_lower = lax.ppermute(kv_mine, "zh", [(0, 1)])
    kv_all = jnp.concatenate([kv_mine, kv_lower], axis=0)
    kv_other = jnp.concatenate([flip_pairs(swap(kv_mine, "c")), flip_pairs(swap(kv_lower, "c"))], axis=0)
    keys = jnp.where(is_key, kv_all, kv_other)
    values = jnp.where(is_key, kv_other, kv_all)
    attended, lse = attention_forward(info, queries, keys, values, low, high)
    branch_parts = dot(attended, attn_out, ((1,), (1,)), BF)
    (branch_attn,) = scatter_sum(branch_parts)

    x_own = tokens.astype(F32)
    scale_one = rms_scale(x_own)
    xhat_one = x_own * scale_one
    resid = x_own + branch_attn
    scale_two = rms_scale(resid)
    xhat_two = resid * scale_two
    (xn_two,) = gather_rows(xhat_two.astype(BF))
    grad_mlp = pick_blocks(slot.astype(jnp.int32), cot_all, valid)

    gate = dot(xn_two, gate_w, ((1,), (0,)))
    up = dot(xn_two, up_w, ((1,), (0,)))
    sigma = jax.nn.sigmoid(gate)
    activated = gate * sigma
    hidden = (activated * up).astype(BF)
    grad_hidden = dot(grad_mlp, down, ((1,), (0,)))
    grad_up_act = (grad_hidden * activated).astype(BF)
    grad_gate_act = (grad_hidden * up * sigma * (1.0 + gate * (1.0 - sigma))).astype(BF)
    scaled_parts = dot(grad_gate_act, gate_w, ((1,), (1,))) + dot(grad_up_act, up_w, ((1,), (1,)))
    scaled_parts = scaled_parts.astype(BF)

    def reduce_outer(partial):
        return lax.psum_scatter(partial, fsdp, scatter_dimension=0, tiled=True)

    outer = dp_axes[0]
    scaled_parts, xn_late, hidden_late = meet(scaled_parts, xn_two, hidden)
    down_sum = reduce_outer(dot(grad_mlp, hidden_late, ((0,), (0,)), BF))
    gate_sum = reduce_outer(dot(xn_late, grad_gate_act, ((0,), (0,)), BF))
    up_sum = reduce_outer(dot(xn_late, grad_up_act, ((0,), (0,)), BF))
    mlp_parts = dot(hidden_late, down, ((1,), (1,)), BF)
    (scaled,) = scatter_sum(scaled_parts)

    grad_final = grad_mlp[:rows].astype(F32)
    grad_resid = grad_final + scale_two * (
        scaled - xhat_two * jnp.mean(scaled * xhat_two, axis=1, keepdims=True)
    )
    def rest(got, keep):
        mine = add_up(got, keep)
        for axis in dp_axes[1:]:
            mine = add_up(*halve(mine, axis))
        return halve(mine, "zh")

    (grad_branch,) = gather_rows(grad_resid.astype(BF))
    grad_branch, mlp_parts = meet(grad_branch, mlp_parts)
    (branch_mlp,) = scatter_sum(mlp_parts)
    final = resid + branch_mlp
    output = final.astype(BF)
    valid_own = valid[:rows]
    squares = [jnp.sum(a * a * valid_own, axis=0) for a in (branch_attn, resid, branch_mlp, final)]

    grad_attn_f32 = dot(grad_branch, attn_out, ((1,), (0,)))
    grad_attn = grad_attn_f32.astype(BF)
    delta = jnp.sum(grad_attn.astype(F32) * attended.astype(F32), axis=1, keepdims=True)
    grad_q, grad_k, grad_v = attention_backward(
        info, queries, keys, values, low, high, lse, delta, grad_attn
    )
    send = jnp.where(is_key, grad_v, grad_k).astype(BF)
    keep = jnp.where(is_key, grad_k, grad_v)
    chip = keep + flip_pairs(swap(send, "c")).astype(F32)
    from_upper = lax.ppermute(chip[count:].astype(BF), "zh", [(1, 0)])
    square_cols = jnp.pad(jnp.stack(squares, axis=1), ((0, 0), (0, BLK - len(squares)))).astype(BF)
    grad_out = jnp.concatenate([dot(grad_branch, attended, ((0,), (0,)), BF), square_cols], axis=1)
    out_sum = reduce_outer(grad_out)
    grad_kv = chip[:count] + from_upper.astype(F32)
    grad_q_proj = rotate(grad_q, cosine, -sine).astype(BF)
    grad_kv_proj = rotate(grad_kv, cosine_kv, -sine_kv).astype(BF)
    grad_proj = jnp.concatenate([grad_q_proj, grad_kv_proj], axis=1)
    grad_xn_one_parts = dot(grad_proj, attn_in, ((1,), (1,)), BF)
    in_got, in_keep = halve(dot(xn_one, grad_proj, ((0,), (0,)), BF), outer)
    scaled, in_got = scatter_sum(grad_xn_one_parts, in_got)
    in_got, in_keep = rest(in_got, in_keep)
    input_grad = grad_resid + scale_one * (
        scaled - xhat_one * jnp.mean(scaled * xhat_one, axis=1, keepdims=True)
    )
    grad_xn_one_parts, down_sum, gate_sum, out_sum, up_sum = meet(
        grad_xn_one_parts, down_sum, gate_sum, out_sum, up_sum
    )
    grad_down_w = deal_rows(down_sum)
    grad_gate_w = deal_rows(gate_sum)
    grad_out_w = deal_rows(out_sum)
    grad_up_w = deal_rows(up_sum)
    grad_in_w = deal_rows(add_up(in_got, in_keep))
    square_sums = jnp.sum(grad_out_w[:, :, HD : HD + 4], axis=1)
    grad_out_w = grad_out_w[:, :, :HD]

    def gain_gradient(*pairs):
        return sum(jnp.sum(ranked(w).astype(F32) * g, axis=(1, 2)) for w, g in pairs)

    grad_attn_norm = gain_gradient((attn_rows, grad_in_w))
    grad_mlp_norm = gain_gradient((w_gate, grad_gate_w), (w_up, grad_up_w))
    gain_one, gain_two = (g.astype(F32)[:, None, None] for g in (attn_norm, mlp_norm))
    grad_in_w, grad_gate_w, grad_up_w = grad_in_w * gain_one, grad_gate_w * gain_two, grad_up_w * gain_two

    valid_count = jnp.sum((block_counts * BLK - trims).astype(F32))
    rms_stats = jnp.sqrt(square_sums / valid_count).T

    def flat(array):
        return array.reshape(weight_rows, -1)

    grad_kv_w = grad_in_w[:, :, HD:].reshape(weight_rows, TPN // 2, 2, HD)
    return (
        output,
        input_grad.astype(BF),
        grad_attn_norm,
        flat(grad_in_w[:, :, :HD]),
        flat(grad_kv_w[:, :, 0]),
        flat(grad_kv_w[:, :, 1]),
        flat(grad_out_w),
        grad_mlp_norm,
        flat(grad_gate_w),
        flat(grad_up_w),
        flat(grad_down_w),
        rms_stats,
    )


def solution(mesh):
    outer = mesh.shape["dp"]
    bits = outer.bit_length() - 1
    dp_axes = tuple(f"x{i}" for i in range(bits))
    names = dp_axes + ("zh",) + TP_AXES
    fine = Mesh(mesh.devices.reshape((2,) * len(names)), names)
    rows, flat = P(names, None), P(names)
    in_specs = (rows, rows, flat, rows, rows, rows, rows, flat, rows, rows, rows, P(), P(), P())
    out_specs = (rows, rows, flat, rows, rows, rows, rows, flat, rows, rows, rows, P(None, names))
    return jax.shard_map(
        functools.partial(shards, dp_axes),
        mesh=fine,
        in_specs=in_specs,
        out_specs=out_specs,
        check_vma=False,
    )
```

```python
import functools
import math

import jax
import jax.numpy as jnp
import numpy as np
from jax import lax
from jax.experimental import pallas as pl
from jax.experimental.pallas import tpu as pltpu
from jax.sharding import Mesh
from jax.sharding import PartitionSpec as P

HD = 256
BLK = 128
EPSILON = 1e-06
THETA = 1000042.0
TP_AXES = ("zl", "y", "c")
TPN = 8
NEG = -1e30
BF = jnp.bfloat16
F32 = jnp.float32


def swap(array, axis):
    return lax.ppermute(array, axis, [(0, 1), (1, 0)])


def dot(left, right, contract, out=F32):
    got = lax.dot_general(left, right, (contract, ((), ())), preferred_element_type=F32)
    return got.astype(out)


def meet(*arrays):
    return lax.optimization_barrier(arrays)


def after(array, token, nought):
    last = token[(slice(-1, None),) * token.ndim].astype(F32) * nought
    return array + last.reshape((1,) * array.ndim).astype(array.dtype)


def gather_rows(own, *others):
    rows = own.shape[0]
    half = rows // 2
    first, second = own[:half], own[half:]
    first_y = swap(first, "y")
    second_z = swap(second, "zl")
    core_own = swap(own, "c")
    if others:
        first_y, second_z, *others = meet(first_y, second_z, *others)
    core_one = swap(jnp.stack([first_y, second_z]), "c")
    first_z = swap(jnp.stack([first, first_y]), "zl")
    second_y = swap(jnp.stack([second, second_z]), "y")
    core_two = swap(jnp.concatenate([first_z, second_y]), "c")
    pieces = [
        own,
        core_own,
        first_y,
        second_y[0],
        core_one[0],
        core_two[2],
        first_z[0],
        second_z,
        core_two[0],
        core_one[1],
        first_z[1],
        second_y[1],
        core_two[1],
        core_two[3],
    ]
    whole = jnp.concatenate(pieces, axis=0).reshape(TPN * rows, own.shape[1])
    return (whole, *others)


def scatter_begin(parts):
    parts = parts.reshape(TPN, -1, parts.shape[1])
    half = parts.shape[1] // 2
    met = swap(parts[1::2], "c").astype(F32)
    total = parts[0::2].astype(F32) + met
    first, second = total[:, :half], total[:, half:]
    got_first = swap(first[1::2].astype(BF), "y")
    got_second = swap(second[2:].astype(BF), "zl")
    return got_first, got_second, first[0::2], second[:2]


def scatter_end(got_first, got_second, first, second):
    first = first + got_first.astype(F32)
    second = second + got_second.astype(F32)
    got_first = swap(first[1].astype(BF), "zl").astype(F32)
    got_second = swap(second[1].astype(BF), "y").astype(F32)
    return jnp.concatenate([first[0] + got_first, second[0] + got_second], axis=0)


def deal_columns(piece):
    rows, _, columns = piece.shape
    return lax.all_to_all(piece, TP_AXES, 1, 0, tiled=True).reshape(rows * TPN, columns)


def in_order(mine, other, axis):
    low = lax.axis_index(axis) == 0
    return jnp.concatenate([jnp.where(low, mine, other), jnp.where(low, other, mine)], axis=0)


def gather_some(mine, axes):
    for axis in axes[:0:-1]:
        mine = in_order(mine, swap(mine, axis), axis)
    return mine, swap(mine, axes[0])


def halve(partial, axis):
    half = partial.shape[0] // 2
    place = lax.axis_index(axis)
    send = lax.dynamic_slice_in_dim(partial, (1 - place) * half, half, 0).astype(BF)
    keep = lax.dynamic_slice_in_dim(partial, place * half, half, 0)
    return swap(send, axis), keep


def add_up(got, keep):
    return keep.astype(F32) + got.astype(F32)


def deal_rows(mine):
    rows = mine.shape[0] // TPN
    low = mine.astype(BF).reshape(TPN, rows, mine.shape[1])
    got = lax.all_to_all(low, TP_AXES, 0, 0, tiled=True)
    return jnp.swapaxes(got, 0, 1).astype(F32)


def slot_of(tile, info):
    return ((tile // TPN) ^ info[1]) * TPN + ((tile % TPN) ^ info[0])


def forward_kernel(info, q_ref, k_ref, v_ref, lo_ref, hi_ref, out_ref, lse_ref, top, total, acc):
    step = pl.program_id(0)
    rows = q_ref.shape[0]
    last = info[1] * TPN + (info[0] ^ step)
    queries = q_ref[...]
    low, high = lo_ref[...], hi_ref[...]
    top[...] = jnp.full_like(top, NEG)
    total[...] = jnp.zeros_like(total)
    acc[...] = jnp.zeros_like(acc)

    def body(tile, carry):
        start = pl.multiple_of(slot_of(tile, info) * rows, rows)
        keys = k_ref[pl.ds(start, rows), :]
        values = v_ref[pl.ds(start, rows), :]
        scores = dot(queries, keys, ((1,), (1,))) * (HD**-0.5)
        place = tile * rows + lax.broadcasted_iota(jnp.int32, scores.shape, 1)
        scores = jnp.where((place >= low) & (place <= high), scores, NEG)
        before = top[...]
        now = jnp.maximum(before, jnp.max(scores, axis=1, keepdims=True))
        prob = jnp.exp(scores - now)
        fade = jnp.exp(before - now)
        top[...] = now
        total[...] = total[...] * fade + jnp.sum(prob, axis=1, keepdims=True)
        acc[...] = acc[...] * fade + dot(prob.astype(BF), values, ((1,), (0,)))
        return carry

    lax.fori_loop(info[2 + step], last + 1, body, 0)
    out_ref[...] = (acc[...] / total[...]).astype(BF)
    lse_ref[...] = top[...] + jnp.log(total[...])


def backward_kernel(
    info, q_ref, k_ref, v_ref, lo_ref, hi_ref, lse_ref, delta_ref, grad_ref, gq_ref, gk_ref, gv_ref, acc
):
    step = pl.program_id(0)
    rows = q_ref.shape[0]
    last = info[1] * TPN + (info[0] ^ step)
    queries, grads = q_ref[...], grad_ref[...]
    low, high = lo_ref[...], hi_ref[...]
    lse, delta = lse_ref[...], delta_ref[...]
    acc[...] = jnp.zeros_like(acc)

    @pl.when(step == 0)
    def _():
        gk_ref[...] = jnp.zeros_like(gk_ref)
        gv_ref[...] = jnp.zeros_like(gv_ref)

    def body(tile, carry):
        start = pl.multiple_of(slot_of(tile, info) * rows, rows)
        keys = k_ref[pl.ds(start, rows), :]
        values = v_ref[pl.ds(start, rows), :]
        scores = dot(queries, keys, ((1,), (1,))) * (HD**-0.5)
        place = tile * rows + lax.broadcasted_iota(jnp.int32, scores.shape, 1)
        scores = jnp.where((place >= low) & (place <= high), scores, NEG)
        prob = jnp.exp(scores - lse)
        dprob = dot(grads, values, ((1,), (1,)))
        dscore = (prob * (dprob - delta)).astype(BF)
        acc[...] += dot(dscore, keys, ((1,), (0,)))
        gk_ref[pl.ds(start, rows), :] += dot(dscore, queries, ((0,), (0,))) * (HD**-0.5)
        gv_ref[pl.ds(start, rows), :] += dot(prob.astype(BF), grads, ((0,), (0,)))
        return carry

    lax.fori_loop(info[2 + step], last + 1, body, 0)
    gq_ref[...] = acc[...] * (HD**-0.5)


def tile_spec(rows, width):
    return pl.BlockSpec((rows, width), lambda i, info: (i, 0))


def whole_spec(rows, width):
    return pl.BlockSpec((rows, width), lambda i, info: (0, 0))


def attention_forward(info, queries, keys, values, low, high):
    count, rows = queries.shape[0], queries.shape[0] // TPN
    span = keys.shape[0]
    return pl.pallas_call(
        forward_kernel,
        grid_spec=pltpu.PrefetchScalarGridSpec(
            num_scalar_prefetch=1,
            grid=(TPN,),
            in_specs=[
                tile_spec(rows, HD),
                whole_spec(span, HD),
                whole_spec(span, HD),
                tile_spec(rows, 1),
                tile_spec(rows, 1),
            ],
            out_specs=[tile_spec(rows, HD), tile_spec(rows, 1)],
            scratch_shapes=[
                pltpu.VMEM((rows, 1), F32),
                pltpu.VMEM((rows, 1), F32),
                pltpu.VMEM((rows, HD), F32),
            ],
        ),
        out_shape=[
            jax.ShapeDtypeStruct((count, HD), BF),
            jax.ShapeDtypeStruct((count, 1), F32),
        ],
        compiler_params=pltpu.CompilerParams(vmem_limit_bytes=40 << 20),
        cost_estimate=pl.CostEstimate(
            flops=4 * count * count * HD, bytes_accessed=8 << 20, transcendentals=count * count
        ),
        name="attend",
    )(info, queries, keys, values, low, high)


def attention_backward(info, queries, keys, values, low, high, lse, delta, grads):
    count, rows = queries.shape[0], queries.shape[0] // TPN
    span = keys.shape[0]
    return pl.pallas_call(
        backward_kernel,
        grid_spec=pltpu.PrefetchScalarGridSpec(
            num_scalar_prefetch=1,
            grid=(TPN,),
            in_specs=[
                tile_spec(rows, HD),
                whole_spec(span, HD),
                whole_spec(span, HD),
                tile_spec(rows, 1),
                tile_spec(rows, 1),
                tile_spec(rows, 1),
                tile_spec(rows, 1),
                tile_spec(rows, HD),
            ],
            out_specs=[tile_spec(rows, HD), whole_spec(span, HD), whole_spec(span, HD)],
            scratch_shapes=[pltpu.VMEM((rows, HD), F32)],
        ),
        out_shape=[
            jax.ShapeDtypeStruct((count, HD), F32),
            jax.ShapeDtypeStruct((span, HD), F32),
            jax.ShapeDtypeStruct((span, HD), F32),
        ],
        compiler_params=pltpu.CompilerParams(vmem_limit_bytes=48 << 20),
        cost_estimate=pl.CostEstimate(
            flops=10 * count * count * HD, bytes_accessed=16 << 20, transcendentals=count * count
        ),
        name="attend_back",
    )(info, queries, keys, values, low, high, lse, delta, grads)


def pick_kernel(index, block_ref, valid_ref, out_ref):
    out_ref[...] = block_ref[...] * valid_ref[...].astype(BF)


def pick_blocks(index, blocks, valid):
    count, width = index.shape[0], blocks.shape[1]
    return pl.pallas_call(
        pick_kernel,
        grid_spec=pltpu.PrefetchScalarGridSpec(
            num_scalar_prefetch=1,
            grid=(count,),
            in_specs=[
                pl.BlockSpec((BLK, width), lambda i, index: (index[i], 0)),
                pl.BlockSpec((BLK, 1), lambda i, index: (i, 0)),
            ],
            out_specs=pl.BlockSpec((BLK, width), lambda i, index: (i, 0)),
        ),
        out_shape=jax.ShapeDtypeStruct((count * BLK, width), BF),
        cost_estimate=pl.CostEstimate(flops=0, bytes_accessed=4 * count * BLK * width, transcendentals=0),
        name="pick",
    )(index, blocks, valid)


def rms_scale(values):
    return lax.rsqrt(jnp.mean(values * values, axis=1, keepdims=True) + EPSILON)


def rotate(values, cosine, sine):
    half = HD // 2
    first, second = values[:, :half], values[:, half:]
    return jnp.concatenate([first * cosine - second * sine, second * cosine + first * sine], axis=1)


def flip_pairs(array):
    tiles = array.reshape(-1, 2, 2 * BLK, array.shape[1])
    return jnp.stack([tiles[:, 1], tiles[:, 0]], axis=1).reshape(array.shape)


def shards(
    dp_axes,
    tokens,
    cotangent,
    attn_norm,
    w_query,
    w_key,
    w_value,
    w_output,
    mlp_norm,
    w_gate,
    w_up,
    w_down,
    block_counts,
    trims,
    block_order,
):
    rows, width = tokens.shape
    count = rows * TPN
    weight_rows = w_gate.shape[0]
    rank = lax.axis_index(TP_AXES)
    upper = lax.axis_index("zh")
    core = lax.axis_index("c")
    group = lax.axis_index(dp_axes)

    nought = jnp.minimum(block_counts[0, 0], 0).astype(F32)

    counts_row = lax.dynamic_slice_in_dim(block_counts, group, 1, 0)[0]
    trim_row = lax.dynamic_slice_in_dim(trims, group, 1, 0)[0]
    order_row = lax.dynamic_slice_in_dim(block_order, group, 1, 0)[0]
    number = counts_row.shape[0]
    earlier = np.tril(np.ones((number, number), np.int32))
    seq_ends = jnp.sum(jnp.asarray(earlier) * counts_row[None, :], axis=1)
    seq_starts = seq_ends - counts_row
    ranks = rank ^ jnp.arange(TPN, dtype=jnp.int32)
    tiles = upper * TPN + ranks
    index = (tiles[:, None] * rows + jnp.arange(rows, dtype=jnp.int32)[None, :]).reshape(-1)
    block = index // BLK
    inside = (block[:, None] >= seq_starts[None, :]) & (block[:, None] < seq_ends[None, :])
    low = jnp.sum(jnp.where(inside, seq_starts[None, :] * BLK, 0), axis=1)
    limit = jnp.sum(jnp.where(inside, (counts_row * BLK - trim_row)[None, :], 0), axis=1)
    position = index - low
    valid = (position < limit).astype(F32)[:, None]
    high = jnp.minimum(index, low + limit - 1)
    info = jnp.concatenate(
        [
            jnp.stack([rank, upper]).astype(jnp.int32),
            (low.reshape(TPN, rows)[:, 0] // rows).astype(jnp.int32),
        ]
    )
    low, high = low[:, None], high[:, None]
    freqs = jnp.exp(jnp.arange(HD // 2, dtype=F32) * (-2.0 * math.log(THETA) / HD))
    angle = position.astype(F32)[:, None] * freqs[None, :]
    cosine, sine = jnp.cos(angle), jnp.sin(angle)
    is_key = core == 0
    cosine_kv = jnp.where(is_key, cosine, 1.0)
    sine_kv = jnp.where(is_key, sine, 0.0)

    def ranked(weight):
        return weight.reshape(weight_rows, TPN, -1)

    def scaled_by(weight, gain):
        return (weight.astype(F32) * gain.astype(F32)[:, None, None]).astype(BF)

    key_value = jnp.stack(
        [w_key.reshape(weight_rows, TPN // 2, HD), w_value.reshape(weight_rows, TPN // 2, HD)], axis=2
    ).reshape(weight_rows, TPN, HD)
    attn_rows = jnp.concatenate([ranked(w_query), key_value], axis=2)
    in_part = deal_columns(scaled_by(attn_rows, attn_norm))
    slots = order_row.shape[0]
    per_rank = rows // BLK
    slot_ids = jnp.arange(slots, dtype=jnp.int32)
    home = (tiles[:, None] * per_rank + jnp.arange(per_rank, dtype=jnp.int32)[None, :]).reshape(-1)
    slot = jnp.sum(jnp.where(order_row[None, :] == home[:, None], slot_ids[None, :], 0), axis=1)
    owner = slot // per_rank
    pick = (((owner % TPN) ^ rank) * 2 + (owner // TPN ^ upper)) * per_rank + slot % per_rank

    def outer_gather(part, other):
        return gather_some(in_order(part, other, "zh"), dp_axes)

    x_low, in_part = gather_rows(tokens, in_part)
    in_zh = swap(in_part, "zh")
    in_mine, in_other = outer_gather(in_part, in_zh)
    x_all = x_low.astype(F32)
    xn_one = (x_all * rms_scale(x_all)).astype(BF)
    fsdp = dp_axes + ("zh",)
    cot_other = swap(cotangent, "zh")
    w_output, w_gate_late, w_up_late, w_down_late, x_low = meet(w_output, w_gate, w_up, w_down, x_low)
    out_part = deal_columns(ranked(w_output))
    gate_part = deal_columns(scaled_by(ranked(w_gate_late), mlp_norm))
    cot_pair = meet(cotangent, cot_other, in_zh, x_low, gate_part)[:2]
    xn_one, in_other = meet(xn_one, in_other)
    (cot_all,) = gather_rows(jnp.concatenate(cot_pair, axis=0))
    attn_in = in_order(in_mine, in_other, dp_axes[0])
    attn_out = lax.all_gather(out_part, fsdp, axis=0, tiled=True)
    gate_w = lax.all_gather(gate_part, fsdp, axis=0, tiled=True)
    up_part = deal_columns(scaled_by(ranked(w_up_late), mlp_norm))
    up_w = lax.all_gather(up_part, fsdp, axis=0, tiled=True)
    down_part = deal_columns(ranked(w_down_late))
    down = lax.all_gather(down_part, fsdp, axis=0, tiled=True)
    projected = dot(xn_one, attn_in, ((1,), (0,)))
    queries = rotate(projected[:, :HD], cosine, sine).astype(BF)
    kv_mine = rotate(projected[:, HD:], cosine_kv, sine_kv).astype(BF)
    kv_lower = lax.ppermute(kv_mine, "zh", [(0, 1)])
    kv_all = jnp.concatenate([kv_mine, kv_lower], axis=0)
    kv_other = jnp.concatenate([flip_pairs(swap(kv_mine, "c")), flip_pairs(swap(kv_lower, "c"))], axis=0)
    keys = jnp.where(is_key, kv_all, kv_other)
    values = jnp.where(is_key, kv_other, kv_all)
    attended, lse = attention_forward(info, queries, keys, values, low, high)
    attended, cot_all, up_part, down_part = meet(attended, cot_all, up_part, down_part)
    branch_parts = dot(attended, attn_out, ((1,), (1,)), BF)
    branch_attn = scatter_end(*scatter_begin(branch_parts))
    grad_mlp = pick_blocks(pick.astype(jnp.int32), cot_all, valid)
    branch_attn, grad_mlp = meet(branch_attn, grad_mlp)

    x_own = tokens.astype(F32)
    scale_one = rms_scale(x_own)
    xhat_one = x_own * scale_one
    resid = x_own + branch_attn
    scale_two = rms_scale(resid)
    xhat_two = resid * scale_two
    (xn_two,) = gather_rows(xhat_two.astype(BF))

    ff_part = w_gate.shape[1] // TPN
    gate = dot(xn_two, gate_w, ((1,), (0,)))
    up = dot(xn_two, up_w, ((1,), (0,)))
    sigma = jax.nn.sigmoid(gate)
    activated = gate * sigma
    hidden = (activated * up).astype(BF)
    outer = dp_axes[0]
    grad_down, sigma = meet(dot(grad_mlp, hidden, ((0,), (0,)), BF), sigma)
    activated = gate * sigma
    down_got, down_keep = halve(grad_down, outer)
    grad_hidden = dot(grad_mlp, down, ((1,), (0,)))
    grad_up_act = (grad_hidden * activated).astype(BF)
    grad_gate_act = (grad_hidden * up * sigma * (1.0 + gate * (1.0 - sigma))).astype(BF)
    scaled_parts = dot(grad_gate_act, gate_w, ((1,), (1,))) + dot(grad_up_act, up_w, ((1,), (1,)))
    scaled_parts = scaled_parts.astype(BF)

    def rest(got, keep):
        mine = add_up(got, keep)
        for axis in dp_axes[1:]:
            mine = add_up(*halve(mine, axis))
        return halve(mine, "zh")

    scaled_parts, xn_late, hidden_late, down_got = meet(scaled_parts, xn_two, hidden, down_got)
    down_got, down_keep = rest(down_got, down_keep)
    scaled = scatter_end(*scatter_begin(scaled_parts))
    gate_got, gate_keep = halve(dot(xn_late, grad_gate_act, ((0,), (0,)), BF), outer)
    up_grad = dot(xn_late, grad_up_act, ((0,), (0,)), BF)
    scaled, gate_keep, up_grad, down_got = meet(scaled, gate_keep, up_grad, down_got)
    mlp_parts = dot(hidden_late, down, ((1,), (1,)), BF)

    grad_final = grad_mlp[:rows].astype(F32)
    grad_resid = grad_final + scale_two * (
        scaled - xhat_two * jnp.mean(scaled * xhat_two, axis=1, keepdims=True)
    )


    grad_low = grad_resid.astype(BF)
    (grad_branch,) = gather_rows(grad_low)
    mlp_parts, grad_branch, gate_got = meet(mlp_parts, grad_branch, gate_got)
    gate_got, gate_keep = rest(gate_got, gate_keep)
    up_got, up_keep = halve(up_grad, outer)
    grad_attn_f32 = dot(grad_branch, attn_out, ((1,), (0,)))
    begun = scatter_begin(mlp_parts)
    grad_attn, keep_first, keep_second = meet(grad_attn_f32.astype(BF), *begun[2:])
    begun = (*begun[:2], keep_first, keep_second)
    delta = jnp.sum(grad_attn.astype(F32) * attended.astype(F32), axis=1, keepdims=True)
    grad_q, grad_k, grad_v = attention_backward(
        info, queries, keys, values, low, high, lse, delta, grad_attn
    )
    grad_q, grad_k, grad_v, gate_got, *begun = meet(grad_q, grad_k, grad_v, gate_got, *begun)
    send = jnp.where(is_key, grad_v, grad_k).astype(BF)
    keep = jnp.where(is_key, grad_k, grad_v)
    chip = keep + flip_pairs(swap(send, "c")).astype(F32)
    from_upper = lax.ppermute(chip[count:].astype(BF), "zh", [(1, 0)])
    branch_mlp = scatter_end(*begun)
    grad_down_w = deal_rows(after(add_up(down_got, down_keep), chip, nought))
    from_upper, up_got, branch_mlp = meet(from_upper, up_got, branch_mlp)
    up_got, up_keep = rest(up_got, up_keep)
    final = resid + branch_mlp
    output = final.astype(BF)
    valid_own = valid[:rows]
    squares = [jnp.sum(a * a * valid_own, axis=0) for a in (branch_attn, resid, branch_mlp, final)]
    square_cols = jnp.pad(jnp.stack(squares, axis=1), ((0, 0), (0, BLK - len(squares)))).astype(BF)
    grad_out = jnp.concatenate([dot(grad_branch, attended, ((0,), (0,)), BF), square_cols], axis=1)
    out_got, out_keep = halve(grad_out, outer)
    grad_kv = chip[:count] + from_upper.astype(F32)
    grad_q_proj = rotate(grad_q, cosine, -sine).astype(BF)
    grad_kv_proj = rotate(grad_kv, cosine_kv, -sine_kv).astype(BF)
    grad_proj = jnp.concatenate([grad_q_proj, grad_kv_proj], axis=1)
    grad_xn_one_parts = dot(grad_proj, attn_in, ((1,), (1,)), BF)
    grad_xn_one_parts, grad_proj, out_got = meet(grad_xn_one_parts, grad_proj, out_got)
    out_got, out_keep = rest(out_got, out_keep)
    in_got, in_keep = halve(dot(xn_one, grad_proj, ((0,), (0,)), BF), outer)
    got_first, got_second, *kept = scatter_begin(grad_xn_one_parts)
    grad_gate_w = deal_rows(after(add_up(gate_got, gate_keep), kept[0], nought))
    got_first, got_second, up_got, in_got = meet(got_first, got_second, up_got, in_got)
    in_got, in_keep = rest(in_got, in_keep)
    scaled = scatter_end(got_first, got_second, *kept)
    scaled, out_got = meet(scaled, out_got)
    input_grad = grad_resid + scale_one * (
        scaled - xhat_one * jnp.mean(scaled * xhat_one, axis=1, keepdims=True)
    )
    grad_up_w = deal_rows(add_up(up_got, up_keep))
    grad_out_w = deal_rows(add_up(out_got, out_keep))
    grad_in_w = deal_rows(add_up(in_got, in_keep))
    square_sums = jnp.sum(grad_out_w[:, :, HD : HD + 4], axis=1)
    grad_out_w = grad_out_w[:, :, :HD]

    def gain_gradient(*pairs):
        return sum(jnp.sum(ranked(w).astype(F32) * g, axis=(1, 2)) for w, g in pairs)

    grad_attn_norm = gain_gradient((attn_rows, grad_in_w))
    grad_mlp_norm = gain_gradient((w_gate, grad_gate_w), (w_up, grad_up_w))
    gain_one, gain_two = (g.astype(F32)[:, None, None] for g in (attn_norm, mlp_norm))
    grad_in_w, grad_gate_w, grad_up_w = grad_in_w * gain_one, grad_gate_w * gain_two, grad_up_w * gain_two

    valid_count = jnp.sum((block_counts * BLK - trims).astype(F32))
    rms_stats = jnp.sqrt(square_sums / valid_count).T

    def flat(array):
        return array.reshape(weight_rows, -1)

    grad_kv_w = grad_in_w[:, :, HD:].reshape(weight_rows, TPN // 2, 2, HD)
    return (
        output,
        input_grad.astype(BF),
        grad_attn_norm,
        flat(grad_in_w[:, :, :HD]),
        flat(grad_kv_w[:, :, 0]),
        flat(grad_kv_w[:, :, 1]),
        flat(grad_out_w),
        grad_mlp_norm,
        flat(grad_gate_w),
        flat(grad_up_w),
        flat(grad_down_w),
        rms_stats,
    )


def solution(mesh):
    outer = mesh.shape["dp"]
    bits = outer.bit_length() - 1
    dp_axes = tuple(f"x{i}" for i in range(bits))
    names = dp_axes + ("zh",) + TP_AXES
    fine = Mesh(mesh.devices.reshape((2,) * len(names)), names)
    rows, flat = P(names, None), P(names)
    in_specs = (rows, rows, flat, rows, rows, rows, rows, flat, rows, rows, rows, P(), P(), P())
    out_specs = (rows, rows, flat, rows, rows, rows, rows, flat, rows, rows, rows, P(None, names))
    return jax.shard_map(
        functools.partial(shards, dp_axes),
        mesh=fine,
        in_specs=in_specs,
        out_specs=out_specs,
        check_vma=False,
    )
```

```python
import functools
import math

import jax
import jax.numpy as jnp
import numpy as np
from jax import lax
from jax.experimental import pallas as pl
from jax.experimental.pallas import tpu as pltpu
from jax.sharding import Mesh
from jax.sharding import PartitionSpec as P

HD = 256
BLK = 128
EPSILON = 1e-06
THETA = 1000042.0
TP_AXES = ("zl", "y", "c")
TPN = 8
NEG = -1e30
BF = jnp.bfloat16
F32 = jnp.float32


def swap(array, axis):
    return lax.ppermute(array, axis, [(0, 1), (1, 0)])


def dot(left, right, contract, out=F32):
    got = lax.dot_general(left, right, (contract, ((), ())), preferred_element_type=F32)
    return got.astype(out)


def meet(*arrays):
    return lax.optimization_barrier(arrays)


def after(array, token, nought):
    last = token[(slice(-1, None),) * token.ndim].astype(F32) * nought
    return array + last.reshape((1,) * array.ndim).astype(array.dtype)


def gather_rows(own, *others):
    rows = own.shape[0]
    half = rows // 2
    first, second = own[:half], own[half:]
    first_y = swap(first, "y")
    second_z = swap(second, "zl")
    core_own = swap(own, "c")
    if others:
        first_y, second_z, *others = meet(first_y, second_z, *others)
    core_one = swap(jnp.stack([first_y, second_z]), "c")
    first_z = swap(jnp.stack([first, first_y]), "zl")
    second_y = swap(jnp.stack([second, second_z]), "y")
    core_two = swap(jnp.concatenate([first_z, second_y]), "c")
    pieces = [
        own,
        core_own,
        first_y,
        second_y[0],
        core_one[0],
        core_two[2],
        first_z[0],
        second_z,
        core_two[0],
        core_one[1],
        first_z[1],
        second_y[1],
        core_two[1],
        core_two[3],
    ]
    whole = jnp.concatenate(pieces, axis=0).reshape(TPN * rows, own.shape[1])
    return (whole, *others)


def scatter_begin(parts):
    parts = parts.reshape(TPN, -1, parts.shape[1])
    half = parts.shape[1] // 2
    met = swap(parts[1::2], "c").astype(F32)
    total = parts[0::2].astype(F32) + met
    first, second = total[:, :half], total[:, half:]
    got_first = swap(first[1::2].astype(BF), "y")
    got_second = swap(second[2:].astype(BF), "zl")
    return got_first, got_second, first[0::2], second[:2]


def scatter_end(got_first, got_second, first, second):
    first = first + got_first.astype(F32)
    second = second + got_second.astype(F32)
    got_first = swap(first[1].astype(BF), "zl").astype(F32)
    got_second = swap(second[1].astype(BF), "y").astype(F32)
    return jnp.concatenate([first[0] + got_first, second[0] + got_second], axis=0)


def deal_columns(piece):
    rows, _, columns = piece.shape
    return lax.all_to_all(piece, TP_AXES, 1, 0, tiled=True).reshape(rows * TPN, columns)


def in_order(mine, other, axis):
    low = lax.axis_index(axis) == 0
    return jnp.concatenate([jnp.where(low, mine, other), jnp.where(low, other, mine)], axis=0)


def gather_some(mine, axes):
    for axis in axes[:0:-1]:
        mine = in_order(mine, swap(mine, axis), axis)
    return mine, swap(mine, axes[0])


def halve(partial, axis):
    half = partial.shape[0] // 2
    place = lax.axis_index(axis)
    send = lax.dynamic_slice_in_dim(partial, (1 - place) * half, half, 0).astype(BF)
    keep = lax.dynamic_slice_in_dim(partial, place * half, half, 0)
    return swap(send, axis), keep


def add_up(got, keep):
    return keep.astype(F32) + got.astype(F32)


def deal_rows(mine):
    rows = mine.shape[0] // TPN
    low = mine.astype(BF).reshape(TPN, rows, mine.shape[1])
    got = lax.all_to_all(low, TP_AXES, 0, 0, tiled=True)
    return jnp.swapaxes(got, 0, 1).astype(F32)


def slot_of(tile, info):
    return ((tile // TPN) ^ info[1]) * TPN + ((tile % TPN) ^ info[0])


def forward_kernel(info, q_ref, k_ref, v_ref, lo_ref, hi_ref, out_ref, lse_ref, top, total, acc):
    step = pl.program_id(0)
    rows = q_ref.shape[0]
    last = info[1] * TPN + (info[0] ^ step)
    queries = q_ref[...]
    low, high = lo_ref[...], hi_ref[...]
    top[...] = jnp.full_like(top, NEG)
    total[...] = jnp.zeros_like(total)
    acc[...] = jnp.zeros_like(acc)

    def body(tile, carry):
        start = pl.multiple_of(slot_of(tile, info) * rows, rows)
        keys = k_ref[pl.ds(start, rows), :]
        values = v_ref[pl.ds(start, rows), :]
        scores = dot(queries, keys, ((1,), (1,))) * (HD**-0.5)
        place = tile * rows + lax.broadcasted_iota(jnp.int32, scores.shape, 1)
        scores = jnp.where((place >= low) & (place <= high), scores, NEG)
        before = top[...]
        now = jnp.maximum(before, jnp.max(scores, axis=1, keepdims=True))
        prob = jnp.exp(scores - now)
        fade = jnp.exp(before - now)
        top[...] = now
        total[...] = total[...] * fade + jnp.sum(prob, axis=1, keepdims=True)
        acc[...] = acc[...] * fade + dot(prob.astype(BF), values, ((1,), (0,)))
        return carry

    lax.fori_loop(info[2 + step], last + 1, body, 0)
    out_ref[...] = (acc[...] / total[...]).astype(BF)
    lse_ref[...] = top[...] + jnp.log(total[...])


def backward_kernel(
    info, q_ref, k_ref, v_ref, lo_ref, hi_ref, lse_ref, delta_ref, grad_ref, gq_ref, gk_ref, gv_ref, acc
):
    step = pl.program_id(0)
    rows = q_ref.shape[0]
    last = info[1] * TPN + (info[0] ^ step)
    queries, grads = q_ref[...], grad_ref[...]
    low, high = lo_ref[...], hi_ref[...]
    lse, delta = lse_ref[...], delta_ref[...]
    acc[...] = jnp.zeros_like(acc)

    @pl.when(step == 0)
    def _():
        gk_ref[...] = jnp.zeros_like(gk_ref)
        gv_ref[...] = jnp.zeros_like(gv_ref)

    def body(tile, carry):
        start = pl.multiple_of(slot_of(tile, info) * rows, rows)
        keys = k_ref[pl.ds(start, rows), :]
        values = v_ref[pl.ds(start, rows), :]
        scores = dot(queries, keys, ((1,), (1,))) * (HD**-0.5)
        place = tile * rows + lax.broadcasted_iota(jnp.int32, scores.shape, 1)
        scores = jnp.where((place >= low) & (place <= high), scores, NEG)
        prob = jnp.exp(scores - lse)
        dprob = dot(grads, values, ((1,), (1,)))
        dscore = (prob * (dprob - delta)).astype(BF)
        acc[...] += dot(dscore, keys, ((1,), (0,)))
        gk_ref[pl.ds(start, rows), :] += dot(dscore, queries, ((0,), (0,))) * (HD**-0.5)
        gv_ref[pl.ds(start, rows), :] += dot(prob.astype(BF), grads, ((0,), (0,)))
        return carry

    lax.fori_loop(info[2 + step], last + 1, body, 0)
    gq_ref[...] = acc[...] * (HD**-0.5)


def tile_spec(rows, width):
    return pl.BlockSpec((rows, width), lambda i, info: (i, 0))


def whole_spec(rows, width):
    return pl.BlockSpec((rows, width), lambda i, info: (0, 0))


def attention_forward(info, queries, keys, values, low, high):
    count, rows = queries.shape[0], queries.shape[0] // TPN
    span = keys.shape[0]
    return pl.pallas_call(
        forward_kernel,
        grid_spec=pltpu.PrefetchScalarGridSpec(
            num_scalar_prefetch=1,
            grid=(TPN,),
            in_specs=[
                tile_spec(rows, HD),
                whole_spec(span, HD),
                whole_spec(span, HD),
                tile_spec(rows, 1),
                tile_spec(rows, 1),
            ],
            out_specs=[tile_spec(rows, HD), tile_spec(rows, 1)],
            scratch_shapes=[
                pltpu.VMEM((rows, 1), F32),
                pltpu.VMEM((rows, 1), F32),
                pltpu.VMEM((rows, HD), F32),
            ],
        ),
        out_shape=[
            jax.ShapeDtypeStruct((count, HD), BF),
            jax.ShapeDtypeStruct((count, 1), F32),
        ],
        compiler_params=pltpu.CompilerParams(vmem_limit_bytes=40 << 20),
        cost_estimate=pl.CostEstimate(
            flops=4 * count * count * HD, bytes_accessed=8 << 20, transcendentals=count * count
        ),
        name="attend",
    )(info, queries, keys, values, low, high)


def attention_backward(info, queries, keys, values, low, high, lse, delta, grads):
    count, rows = queries.shape[0], queries.shape[0] // TPN
    span = keys.shape[0]
    return pl.pallas_call(
        backward_kernel,
        grid_spec=pltpu.PrefetchScalarGridSpec(
            num_scalar_prefetch=1,
            grid=(TPN,),
            in_specs=[
                tile_spec(rows, HD),
                whole_spec(span, HD),
                whole_spec(span, HD),
                tile_spec(rows, 1),
                tile_spec(rows, 1),
                tile_spec(rows, 1),
                tile_spec(rows, 1),
                tile_spec(rows, HD),
            ],
            out_specs=[tile_spec(rows, HD), whole_spec(span, HD), whole_spec(span, HD)],
            scratch_shapes=[pltpu.VMEM((rows, HD), F32)],
        ),
        out_shape=[
            jax.ShapeDtypeStruct((count, HD), F32),
            jax.ShapeDtypeStruct((span, HD), F32),
            jax.ShapeDtypeStruct((span, HD), F32),
        ],
        compiler_params=pltpu.CompilerParams(vmem_limit_bytes=48 << 20),
        cost_estimate=pl.CostEstimate(
            flops=10 * count * count * HD, bytes_accessed=16 << 20, transcendentals=count * count
        ),
        name="attend_back",
    )(info, queries, keys, values, low, high, lse, delta, grads)


def mlp_kernel(x_ref, cot_ref, wg_ref, wu_ref, wd_ref, hidden_ref, gate_ref, up_ref, out_ref, back_ref):
    gate = dot(x_ref[...], wg_ref[...], ((1,), (0,)))
    up = dot(x_ref[...], wu_ref[...], ((1,), (0,)))
    sigma = jax.nn.sigmoid(gate)
    activated = gate * sigma
    hidden = (activated * up).astype(BF)
    hidden_ref[...] = hidden
    grad = dot(cot_ref[...], wd_ref[...], ((1,), (0,)))
    up_act = (grad * activated).astype(BF)
    gate_act = (grad * up * sigma * (1.0 + gate * (1.0 - sigma))).astype(BF)
    gate_ref[...], up_ref[...] = gate_act, up_act
    out_ref[...] = dot(hidden, wd_ref[...], ((1,), (1,)), BF)
    back = dot(gate_act, wg_ref[...], ((1,), (1,))) + dot(up_act, wu_ref[...], ((1,), (1,)))
    back_ref[...] = back.astype(BF)


def feed_forward(normed, cotangent, w_gate, w_up, w_down):
    count, width = normed.shape
    part = w_gate.shape[1]
    rows = count // TPN
    wide = pl.BlockSpec((rows, width), lambda i: (i, 0))
    narrow = pl.BlockSpec((rows, part), lambda i: (i, 0))
    weight = pl.BlockSpec((width, part), lambda i: (0, 0), pipeline_mode=pl.Buffered(1))
    return pl.pallas_call(
        mlp_kernel,
        grid=(TPN,),
        in_specs=[wide, wide, weight, weight, weight],
        out_specs=[narrow, narrow, narrow, wide, wide],
        out_shape=[jax.ShapeDtypeStruct((count, part), BF)] * 3 + [jax.ShapeDtypeStruct((count, width), BF)] * 2,
        compiler_params=pltpu.CompilerParams(vmem_limit_bytes=56 << 20),
        cost_estimate=pl.CostEstimate(
            flops=12 * count * width * part, bytes_accessed=60 << 20, transcendentals=count * part
        ),
        name="mlp",
    )(normed, cotangent, w_gate, w_up, w_down)


def pick_kernel(index, block_ref, valid_ref, out_ref):
    out_ref[...] = block_ref[...] * valid_ref[...].astype(BF)


def pick_blocks(index, blocks, valid):
    count, width = index.shape[0], blocks.shape[1]
    return pl.pallas_call(
        pick_kernel,
        grid_spec=pltpu.PrefetchScalarGridSpec(
            num_scalar_prefetch=1,
            grid=(count,),
            in_specs=[
                pl.BlockSpec((BLK, width), lambda i, index: (index[i], 0)),
                pl.BlockSpec((BLK, 1), lambda i, index: (i, 0)),
            ],
            out_specs=pl.BlockSpec((BLK, width), lambda i, index: (i, 0)),
        ),
        out_shape=jax.ShapeDtypeStruct((count * BLK, width), BF),
        cost_estimate=pl.CostEstimate(flops=0, bytes_accessed=4 * count * BLK * width, transcendentals=0),
        name="pick",
    )(index, blocks, valid)


def rms_scale(values):
    return lax.rsqrt(jnp.mean(values * values, axis=1, keepdims=True) + EPSILON)


def rotate(values, cosine, sine):
    half = HD // 2
    first, second = values[:, :half], values[:, half:]
    return jnp.concatenate([first * cosine - second * sine, second * cosine + first * sine], axis=1)


def flip_pairs(array):
    tiles = array.reshape(-1, 2, 2 * BLK, array.shape[1])
    return jnp.stack([tiles[:, 1], tiles[:, 0]], axis=1).reshape(array.shape)


def shards(
    dp_axes,
    tokens,
    cotangent,
    attn_norm,
    w_query,
    w_key,
    w_value,
    w_output,
    mlp_norm,
    w_gate,
    w_up,
    w_down,
    block_counts,
    trims,
    block_order,
):
    rows, width = tokens.shape
    count = rows * TPN
    weight_rows = w_gate.shape[0]
    rank = lax.axis_index(TP_AXES)
    upper = lax.axis_index("zh")
    core = lax.axis_index("c")
    group = lax.axis_index(dp_axes)

    nought = jnp.minimum(block_counts[0, 0], 0).astype(F32)

    counts_row = lax.dynamic_slice_in_dim(block_counts, group, 1, 0)[0]
    trim_row = lax.dynamic_slice_in_dim(trims, group, 1, 0)[0]
    order_row = lax.dynamic_slice_in_dim(block_order, group, 1, 0)[0]
    number = counts_row.shape[0]
    earlier = np.tril(np.ones((number, number), np.int32))
    seq_ends = jnp.sum(jnp.asarray(earlier) * counts_row[None, :], axis=1)
    seq_starts = seq_ends - counts_row
    ranks = rank ^ jnp.arange(TPN, dtype=jnp.int32)
    tiles = upper * TPN + ranks
    index = (tiles[:, None] * rows + jnp.arange(rows, dtype=jnp.int32)[None, :]).reshape(-1)
    block = index // BLK
    inside = (block[:, None] >= seq_starts[None, :]) & (block[:, None] < seq_ends[None, :])
    low = jnp.sum(jnp.where(inside, seq_starts[None, :] * BLK, 0), axis=1)
    limit = jnp.sum(jnp.where(inside, (counts_row * BLK - trim_row)[None, :], 0), axis=1)
    position = index - low
    valid = (position < limit).astype(F32)[:, None]
    high = jnp.minimum(index, low + limit - 1)
    info = jnp.concatenate(
        [
            jnp.stack([rank, upper]).astype(jnp.int32),
            (low.reshape(TPN, rows)[:, 0] // rows).astype(jnp.int32),
        ]
    )
    low, high = low[:, None], high[:, None]
    freqs = jnp.exp(jnp.arange(HD // 2, dtype=F32) * (-2.0 * math.log(THETA) / HD))
    angle = position.astype(F32)[:, None] * freqs[None, :]
    cosine, sine = jnp.cos(angle), jnp.sin(angle)
    is_key = core == 0
    cosine_kv = jnp.where(is_key, cosine, 1.0)
    sine_kv = jnp.where(is_key, sine, 0.0)

    def ranked(weight):
        return weight.reshape(weight_rows, TPN, -1)

    def scaled_by(weight, gain):
        return (weight.astype(F32) * gain.astype(F32)[:, None, None]).astype(BF)

    key_value = jnp.stack(
        [w_key.reshape(weight_rows, TPN // 2, HD), w_value.reshape(weight_rows, TPN // 2, HD)], axis=2
    ).reshape(weight_rows, TPN, HD)
    attn_rows = jnp.concatenate([ranked(w_query), key_value], axis=2)
    in_part = deal_columns(scaled_by(attn_rows, attn_norm))
    slots = order_row.shape[0]
    per_rank = rows // BLK
    slot_ids = jnp.arange(slots, dtype=jnp.int32)
    home = (tiles[:, None] * per_rank + jnp.arange(per_rank, dtype=jnp.int32)[None, :]).reshape(-1)
    slot = jnp.sum(jnp.where(order_row[None, :] == home[:, None], slot_ids[None, :], 0), axis=1)
    owner = slot // per_rank
    pick = (((owner % TPN) ^ rank) * 2 + (owner // TPN ^ upper)) * per_rank + slot % per_rank

    def outer_gather(part, other):
        return gather_some(in_order(part, other, "zh"), dp_axes)

    x_low, in_part = gather_rows(tokens, in_part)
    in_zh = swap(in_part, "zh")
    in_mine, in_other = outer_gather(in_part, in_zh)
    x_all = x_low.astype(F32)
    xn_one = (x_all * rms_scale(x_all)).astype(BF)
    fsdp = dp_axes + ("zh",)
    cot_other = swap(cotangent, "zh")
    w_output, w_gate_late, w_up_late, w_down_late, x_low = meet(w_output, w_gate, w_up, w_down, x_low)
    out_part = deal_columns(ranked(w_output))
    gate_part = deal_columns(scaled_by(ranked(w_gate_late), mlp_norm))
    cot_pair = meet(cotangent, cot_other, in_zh, x_low, gate_part)[:2]
    xn_one, in_other = meet(xn_one, in_other)
    (cot_all,) = gather_rows(jnp.concatenate(cot_pair, axis=0))
    attn_in = in_order(in_mine, in_other, dp_axes[0])
    gate_half = lax.all_gather(gate_part, "zh", axis=0, tiled=True)
    attn_out = lax.all_gather(out_part, fsdp, axis=0, tiled=True)
    up_part = deal_columns(scaled_by(ranked(w_up_late), mlp_norm))
    up_half = lax.all_gather(up_part, "zh", axis=0, tiled=True)
    down_part = deal_columns(ranked(w_down_late))
    projected = dot(xn_one, attn_in, ((1,), (0,)))
    queries = rotate(projected[:, :HD], cosine, sine).astype(BF)
    kv_mine = rotate(projected[:, HD:], cosine_kv, sine_kv).astype(BF)
    kv_lower = lax.ppermute(kv_mine, "zh", [(0, 1)])
    kv_lower, gate_half = meet(kv_lower, gate_half)
    gate_mine, gate_other = gather_some(gate_half, dp_axes)
    kv_all = jnp.concatenate([kv_mine, kv_lower], axis=0)
    kv_other = jnp.concatenate([flip_pairs(swap(kv_mine, "c")), flip_pairs(swap(kv_lower, "c"))], axis=0)
    keys = jnp.where(is_key, kv_all, kv_other)
    values = jnp.where(is_key, kv_other, kv_all)
    attended, lse = attention_forward(info, queries, keys, values, low, high)
    attended, cot_all, gate_other, up_half, down_part = meet(attended, cot_all, gate_other, up_half, down_part)
    down_half = lax.all_gather(down_part, "zh", axis=0, tiled=True)
    up_mine, up_other = gather_some(up_half, dp_axes)
    branch_parts = dot(attended, attn_out, ((1,), (1,)), BF)
    got_first, got_second, *kept = scatter_begin(branch_parts)
    got_first, got_second, down_half = meet(got_first, got_second, down_half)
    down_mine, down_other = gather_some(down_half, dp_axes)
    branch_attn = scatter_end(got_first, got_second, *kept)
    grad_mlp = pick_blocks(pick.astype(jnp.int32), cot_all, valid)
    branch_attn, grad_mlp, up_other = meet(branch_attn, grad_mlp, up_other)
    gate_w = in_order(gate_mine, gate_other, dp_axes[0])

    x_own = tokens.astype(F32)
    scale_one = rms_scale(x_own)
    xhat_one = x_own * scale_one
    resid = x_own + branch_attn
    scale_two = rms_scale(resid)
    xhat_two = resid * scale_two
    up_w = in_order(up_mine, up_other, dp_axes[0])
    xn_two, down_other = gather_rows(xhat_two.astype(BF), down_other)
    down = in_order(down_mine, down_other, dp_axes[0])

    ff_part = w_gate.shape[1] // TPN
    outer = dp_axes[0]
    hidden, grad_gate_act, grad_up_act, mlp_parts, scaled_parts = feed_forward(xn_two, grad_mlp, gate_w, up_w, down)

    def rest(got, keep):
        mine = add_up(got, keep)
        for axis in dp_axes[1:]:
            mine = add_up(*halve(mine, axis))
        return halve(mine, "zh")

    got_first, got_second, *kept = scatter_begin(scaled_parts)
    down_got, down_keep = halve(dot(grad_mlp, hidden, ((0,), (0,)), BF), outer)
    gate_got, gate_keep = halve(dot(xn_two, grad_gate_act, ((0,), (0,)), BF), outer)
    up_grad = dot(xn_two, grad_up_act, ((0,), (0,)), BF)
    got_first, got_second, down_got = meet(got_first, got_second, down_got)
    down_got, down_keep = rest(down_got, down_keep)
    scaled = scatter_end(got_first, got_second, *kept)
    scaled, gate_keep, up_grad = meet(scaled, gate_keep, up_grad)

    grad_final = grad_mlp[:rows].astype(F32)
    grad_resid = grad_final + scale_two * (
        scaled - xhat_two * jnp.mean(scaled * xhat_two, axis=1, keepdims=True)
    )


    grad_low = grad_resid.astype(BF)
    grad_branch, down_got, gate_got = gather_rows(grad_low, down_got, gate_got)
    mlp_parts, grad_branch = meet(mlp_parts, grad_branch)
    gate_got, gate_keep = rest(gate_got, gate_keep)
    up_got, up_keep = halve(up_grad, outer)
    grad_attn_f32 = dot(grad_branch, attn_out, ((1,), (0,)))
    begun = scatter_begin(mlp_parts)
    grad_attn, keep_first, keep_second = meet(grad_attn_f32.astype(BF), *begun[2:])
    begun = (*begun[:2], keep_first, keep_second)
    delta = jnp.sum(grad_attn.astype(F32) * attended.astype(F32), axis=1, keepdims=True)
    grad_q, grad_k, grad_v = attention_backward(
        info, queries, keys, values, low, high, lse, delta, grad_attn
    )
    grad_q, grad_k, grad_v, gate_got, *begun = meet(grad_q, grad_k, grad_v, gate_got, *begun)
    send = jnp.where(is_key, grad_v, grad_k).astype(BF)
    keep = jnp.where(is_key, grad_k, grad_v)
    chip = keep + flip_pairs(swap(send, "c")).astype(F32)
    from_upper = lax.ppermute(chip[count:].astype(BF), "zh", [(1, 0)])
    branch_mlp = scatter_end(*begun)
    grad_down_w = deal_rows(after(add_up(down_got, down_keep), chip, nought))
    from_upper, up_got, branch_mlp = meet(from_upper, up_got, branch_mlp)
    up_got, up_keep = rest(up_got, up_keep)
    final = resid + branch_mlp
    output = final.astype(BF)
    valid_own = valid[:rows]
    squares = [jnp.sum(a * a * valid_own, axis=0) for a in (branch_attn, resid, branch_mlp, final)]
    square_cols = jnp.pad(jnp.stack(squares, axis=1), ((0, 0), (0, BLK - len(squares)))).astype(BF)
    grad_out = jnp.concatenate([dot(grad_branch, attended, ((0,), (0,)), BF), square_cols], axis=1)
    out_got, out_keep = halve(grad_out, outer)
    grad_kv = chip[:count] + from_upper.astype(F32)
    grad_q_proj = rotate(grad_q, cosine, -sine).astype(BF)
    grad_kv_proj = rotate(grad_kv, cosine_kv, -sine_kv).astype(BF)
    grad_proj = jnp.concatenate([grad_q_proj, grad_kv_proj], axis=1)
    grad_xn_one_parts = dot(grad_proj, attn_in, ((1,), (1,)), BF)
    grad_xn_one_parts, grad_proj, out_got = meet(grad_xn_one_parts, grad_proj, out_got)
    out_got, out_keep = rest(out_got, out_keep)
    in_got, in_keep = halve(dot(xn_one, grad_proj, ((0,), (0,)), BF), outer)
    got_first, got_second, *kept = scatter_begin(grad_xn_one_parts)
    grad_gate_w = deal_rows(after(add_up(gate_got, gate_keep), kept[0], nought))
    got_first, got_second, up_got, in_got = meet(got_first, got_second, up_got, in_got)
    in_got, in_keep = rest(in_got, in_keep)
    scaled = scatter_end(got_first, got_second, *kept)
    scaled, out_got = meet(scaled, out_got)
    input_grad = grad_resid + scale_one * (
        scaled - xhat_one * jnp.mean(scaled * xhat_one, axis=1, keepdims=True)
    )
    grad_up_w = deal_rows(add_up(up_got, up_keep))
    grad_out_w = deal_rows(add_up(out_got, out_keep))
    grad_in_w = deal_rows(add_up(in_got, in_keep))
    square_sums = jnp.sum(grad_out_w[:, :, HD : HD + 4], axis=1)
    grad_out_w = grad_out_w[:, :, :HD]

    def gain_gradient(*pairs):
        return sum(jnp.sum(ranked(w).astype(F32) * g, axis=(1, 2)) for w, g in pairs)

    grad_attn_norm = gain_gradient((attn_rows, grad_in_w))
    grad_mlp_norm = gain_gradient((w_gate, grad_gate_w), (w_up, grad_up_w))
    gain_one, gain_two = (g.astype(F32)[:, None, None] for g in (attn_norm, mlp_norm))
    grad_in_w, grad_gate_w, grad_up_w = grad_in_w * gain_one, grad_gate_w * gain_two, grad_up_w * gain_two

    valid_count = jnp.sum((block_counts * BLK - trims).astype(F32))
    rms_stats = jnp.sqrt(square_sums / valid_count).T

    def flat(array):
        return array.reshape(weight_rows, -1)

    grad_kv_w = grad_in_w[:, :, HD:].reshape(weight_rows, TPN // 2, 2, HD)
    return (
        output,
        input_grad.astype(BF),
        grad_attn_norm,
        flat(grad_in_w[:, :, :HD]),
        flat(grad_kv_w[:, :, 0]),
        flat(grad_kv_w[:, :, 1]),
        flat(grad_out_w),
        grad_mlp_norm,
        flat(grad_gate_w),
        flat(grad_up_w),
        flat(grad_down_w),
        rms_stats,
    )


def solution(mesh):
    outer = mesh.shape["dp"]
    bits = outer.bit_length() - 1
    dp_axes = tuple(f"x{i}" for i in range(bits))
    names = dp_axes + ("zh",) + TP_AXES
    fine = Mesh(mesh.devices.reshape((2,) * len(names)), names)
    rows, flat = P(names, None), P(names)
    in_specs = (rows, rows, flat, rows, rows, rows, rows, flat, rows, rows, rows, P(), P(), P())
    out_specs = (rows, rows, flat, rows, rows, rows, rows, flat, rows, rows, rows, P(None, names))
    return jax.shard_map(
        functools.partial(shards, dp_axes),
        mesh=fine,
        in_specs=in_specs,
        out_specs=out_specs,
        check_vma=False,
    )
```

```python
import functools
import math

import jax
import jax.numpy as jnp
import numpy as np
from jax import lax
from jax.experimental import pallas as pl
from jax.experimental.pallas import tpu as pltpu
from jax.sharding import Mesh
from jax.sharding import PartitionSpec as P

HD = 256
BLK = 128
EPSILON = 1e-06
THETA = 1000042.0
TP_AXES = ("zl", "y", "c")
TPN = 8
NEG = -1e30
BF = jnp.bfloat16
F32 = jnp.float32


def swap(array, axis):
    return lax.ppermute(array, axis, [(0, 1), (1, 0)])


def dot(left, right, contract, out=F32):
    got = lax.dot_general(left, right, (contract, ((), ())), preferred_element_type=F32)
    return got.astype(out)


def meet(*arrays):
    return lax.optimization_barrier(arrays)


def after(array, token, nought):
    last = token[(slice(-1, None),) * token.ndim].astype(F32) * nought
    return array + last.reshape((1,) * array.ndim).astype(array.dtype)


def gather_rows(own, *others, last=None):
    rows = own.shape[0]
    half = rows // 2
    first, second = own[:half], own[half:]
    first_y = swap(first, "y")
    second_z = swap(second, "zl")
    core_own = swap(own, "c")
    if others:
        first_y, second_z, *others = meet(first_y, second_z, *others)
    core_one = swap(jnp.stack([first_y, second_z]), "c")
    first_z = swap(jnp.stack([first, first_y]), "zl")
    second_y = swap(jnp.stack([second, second_z]), "y")
    if last is not None:
        first_z, second_y, last = meet(first_z, second_y, last)
        others = (*others, last)
    core_two = swap(jnp.concatenate([first_z, second_y]), "c")
    pieces = [
        own,
        core_own,
        first_y,
        second_y[0],
        core_one[0],
        core_two[2],
        first_z[0],
        second_z,
        core_two[0],
        core_one[1],
        first_z[1],
        second_y[1],
        core_two[1],
        core_two[3],
    ]
    whole = jnp.concatenate(pieces, axis=0).reshape(TPN * rows, own.shape[1])
    return (whole, *others)


def core_sum(parts):
    parts = parts.reshape(TPN, -1, parts.shape[1])
    return parts[0::2].astype(F32) + swap(parts[1::2], "c").astype(F32)


def scatter_begin(total):
    half = total.shape[1] // 2
    first, second = total[:, :half], total[:, half:]
    got_first = swap(first[1::2].astype(BF), "y")
    got_second = swap(second[2:].astype(BF), "zl")
    return got_first, got_second, first[0::2], second[:2]


def scatter_end(got_first, got_second, first, second):
    first = first + got_first.astype(F32)
    second = second + got_second.astype(F32)
    got_first = swap(first[1].astype(BF), "zl").astype(F32)
    got_second = swap(second[1].astype(BF), "y").astype(F32)
    return jnp.concatenate([first[0] + got_first, second[0] + got_second], axis=0)


def deal_columns(piece):
    rows, _, columns = piece.shape
    return lax.all_to_all(piece, TP_AXES, 1, 0, tiled=True).reshape(rows * TPN, columns)


def in_order(mine, other, axis):
    low = lax.axis_index(axis) == 0
    return jnp.concatenate([jnp.where(low, mine, other), jnp.where(low, other, mine)], axis=0)


def gather_some(mine, axes):
    for axis in axes[:0:-1]:
        mine = in_order(mine, swap(mine, axis), axis)
    return mine, swap(mine, axes[0])


def halve(partial, axis):
    half = partial.shape[0] // 2
    place = lax.axis_index(axis)
    send = lax.dynamic_slice_in_dim(partial, (1 - place) * half, half, 0).astype(BF)
    keep = lax.dynamic_slice_in_dim(partial, place * half, half, 0)
    return swap(send, axis), keep


def add_up(got, keep):
    return keep.astype(F32) + got.astype(F32)


def deal_rows(mine):
    rows = mine.shape[0] // TPN
    low = mine.astype(BF).reshape(TPN, rows, mine.shape[1])
    got = lax.all_to_all(low, TP_AXES, 0, 0, tiled=True)
    return jnp.swapaxes(got, 0, 1).astype(F32)


def slot_of(tile, info):
    return ((tile // TPN) ^ info[1]) * TPN + ((tile % TPN) ^ info[0])


def forward_kernel(info, q_ref, k_ref, v_ref, lo_ref, hi_ref, out_ref, lse_ref, top, total, acc):
    step = pl.program_id(0)
    rows = q_ref.shape[0]
    last = info[1] * TPN + (info[0] ^ step)
    queries = q_ref[...]
    low, high = lo_ref[...], hi_ref[...]
    top[...] = jnp.full_like(top, NEG)
    total[...] = jnp.zeros_like(total)
    acc[...] = jnp.zeros_like(acc)

    def body(tile, carry):
        start = pl.multiple_of(slot_of(tile, info) * rows, rows)
        keys = k_ref[pl.ds(start, rows), :]
        values = v_ref[pl.ds(start, rows), :]
        scores = dot(queries, keys, ((1,), (1,))) * (HD**-0.5)
        place = tile * rows + lax.broadcasted_iota(jnp.int32, scores.shape, 1)
        scores = jnp.where((place >= low) & (place <= high), scores, NEG)
        before = top[...]
        now = jnp.maximum(before, jnp.max(scores, axis=1, keepdims=True))
        prob = jnp.exp(scores - now)
        fade = jnp.exp(before - now)
        top[...] = now
        total[...] = total[...] * fade + jnp.sum(prob, axis=1, keepdims=True)
        acc[...] = acc[...] * fade + dot(prob.astype(BF), values, ((1,), (0,)))
        return carry

    lax.fori_loop(info[2 + step], last + 1, body, 0)
    out_ref[...] = (acc[...] / total[...]).astype(BF)
    lse_ref[...] = top[...] + jnp.log(total[...])


def backward_kernel(
    info, q_ref, k_ref, v_ref, lo_ref, hi_ref, lse_ref, delta_ref, grad_ref, gq_ref, gk_ref, gv_ref, acc
):
    step = pl.program_id(0)
    rows = q_ref.shape[0]
    last = info[1] * TPN + (info[0] ^ step)
    queries, grads = q_ref[...], grad_ref[...]
    low, high = lo_ref[...], hi_ref[...]
    lse, delta = lse_ref[...], delta_ref[...]
    acc[...] = jnp.zeros_like(acc)

    @pl.when(step == 0)
    def _():
        gk_ref[...] = jnp.zeros_like(gk_ref)
        gv_ref[...] = jnp.zeros_like(gv_ref)

    def body(tile, carry):
        start = pl.multiple_of(slot_of(tile, info) * rows, rows)
        keys = k_ref[pl.ds(start, rows), :]
        values = v_ref[pl.ds(start, rows), :]
        scores = dot(queries, keys, ((1,), (1,))) * (HD**-0.5)
        place = tile * rows + lax.broadcasted_iota(jnp.int32, scores.shape, 1)
        scores = jnp.where((place >= low) & (place <= high), scores, NEG)
        prob = jnp.exp(scores - lse)
        dprob = dot(grads, values, ((1,), (1,)))
        dscore = (prob * (dprob - delta)).astype(BF)
        acc[...] += dot(dscore, keys, ((1,), (0,)))
        gk_ref[pl.ds(start, rows), :] += dot(dscore, queries, ((0,), (0,))) * (HD**-0.5)
        gv_ref[pl.ds(start, rows), :] += dot(prob.astype(BF), grads, ((0,), (0,)))
        return carry

    lax.fori_loop(info[2 + step], last + 1, body, 0)
    gq_ref[...] = acc[...] * (HD**-0.5)


def tile_spec(rows, width):
    return pl.BlockSpec((rows, width), lambda i, info: (i, 0))


def whole_spec(rows, width):
    return pl.BlockSpec((rows, width), lambda i, info: (0, 0))


def attention_forward(info, queries, keys, values, low, high):
    count, rows = queries.shape[0], queries.shape[0] // TPN
    span = keys.shape[0]
    return pl.pallas_call(
        forward_kernel,
        grid_spec=pltpu.PrefetchScalarGridSpec(
            num_scalar_prefetch=1,
            grid=(TPN,),
            in_specs=[
                tile_spec(rows, HD),
                whole_spec(span, HD),
                whole_spec(span, HD),
                tile_spec(rows, 1),
                tile_spec(rows, 1),
            ],
            out_specs=[tile_spec(rows, HD), tile_spec(rows, 1)],
            scratch_shapes=[
                pltpu.VMEM((rows, 1), F32),
                pltpu.VMEM((rows, 1), F32),
                pltpu.VMEM((rows, HD), F32),
            ],
        ),
        out_shape=[
            jax.ShapeDtypeStruct((count, HD), BF),
            jax.ShapeDtypeStruct((count, 1), F32),
        ],
        compiler_params=pltpu.CompilerParams(vmem_limit_bytes=40 << 20),
        cost_estimate=pl.CostEstimate(
            flops=4 * count * count * HD, bytes_accessed=8 << 20, transcendentals=count * count
        ),
        name="attend",
    )(info, queries, keys, values, low, high)


def attention_backward(info, queries, keys, values, low, high, lse, delta, grads):
    count, rows = queries.shape[0], queries.shape[0] // TPN
    span = keys.shape[0]
    return pl.pallas_call(
        backward_kernel,
        grid_spec=pltpu.PrefetchScalarGridSpec(
            num_scalar_prefetch=1,
            grid=(TPN,),
            in_specs=[
                tile_spec(rows, HD),
                whole_spec(span, HD),
                whole_spec(span, HD),
                tile_spec(rows, 1),
                tile_spec(rows, 1),
                tile_spec(rows, 1),
                tile_spec(rows, 1),
                tile_spec(rows, HD),
            ],
            out_specs=[tile_spec(rows, HD), whole_spec(span, HD), whole_spec(span, HD)],
            scratch_shapes=[pltpu.VMEM((rows, HD), F32)],
        ),
        out_shape=[
            jax.ShapeDtypeStruct((count, HD), F32),
            jax.ShapeDtypeStruct((span, HD), F32),
            jax.ShapeDtypeStruct((span, HD), F32),
        ],
        compiler_params=pltpu.CompilerParams(vmem_limit_bytes=48 << 20),
        cost_estimate=pl.CostEstimate(
            flops=10 * count * count * HD, bytes_accessed=16 << 20, transcendentals=count * count
        ),
        name="attend_back",
    )(info, queries, keys, values, low, high, lse, delta, grads)


def mlp_kernel(x_ref, cot_ref, wg_ref, wu_ref, wd_ref, hidden_ref, gate_ref, up_ref, out_ref, back_ref):
    gate = dot(x_ref[...], wg_ref[...], ((1,), (0,)))
    up = dot(x_ref[...], wu_ref[...], ((1,), (0,)))
    sigma = jax.nn.sigmoid(gate)
    activated = gate * sigma
    hidden = (activated * up).astype(BF)
    hidden_ref[...] = hidden
    grad = dot(cot_ref[...], wd_ref[...], ((1,), (0,)))
    up_act = (grad * activated).astype(BF)
    gate_act = (grad * up * sigma * (1.0 + gate * (1.0 - sigma))).astype(BF)
    gate_ref[...], up_ref[...] = gate_act, up_act
    out_ref[...] = dot(hidden, wd_ref[...], ((1,), (1,)), BF)
    back = dot(gate_act, wg_ref[...], ((1,), (1,))) + dot(up_act, wu_ref[...], ((1,), (1,)))
    back_ref[...] = back.astype(BF)


def feed_forward(normed, cotangent, w_gate, w_up, w_down):
    count, width = normed.shape
    part = w_gate.shape[1]
    rows = count // TPN
    wide = pl.BlockSpec((rows, width), lambda i: (i, 0))
    narrow = pl.BlockSpec((rows, part), lambda i: (i, 0))
    weight = pl.BlockSpec((width, part), lambda i: (0, 0), pipeline_mode=pl.Buffered(1))
    return pl.pallas_call(
        mlp_kernel,
        grid=(TPN,),
        in_specs=[wide, wide, weight, weight, weight],
        out_specs=[narrow, narrow, narrow, wide, wide],
        out_shape=[jax.ShapeDtypeStruct((count, part), BF)] * 3 + [jax.ShapeDtypeStruct((count, width), BF)] * 2,
        compiler_params=pltpu.CompilerParams(vmem_limit_bytes=56 << 20),
        cost_estimate=pl.CostEstimate(
            flops=12 * count * width * part, bytes_accessed=60 << 20, transcendentals=count * part
        ),
        name="mlp",
    )(normed, cotangent, w_gate, w_up, w_down)


def pick_kernel(index, block_ref, valid_ref, out_ref):
    out_ref[...] = block_ref[...] * valid_ref[...].astype(BF)


def pick_blocks(index, blocks, valid):
    count, width = index.shape[0], blocks.shape[1]
    return pl.pallas_call(
        pick_kernel,
        grid_spec=pltpu.PrefetchScalarGridSpec(
            num_scalar_prefetch=1,
            grid=(count,),
            in_specs=[
                pl.BlockSpec((BLK, width), lambda i, index: (index[i], 0)),
                pl.BlockSpec((BLK, 1), lambda i, index: (i, 0)),
            ],
            out_specs=pl.BlockSpec((BLK, width), lambda i, index: (i, 0)),
        ),
        out_shape=jax.ShapeDtypeStruct((count * BLK, width), BF),
        cost_estimate=pl.CostEstimate(flops=0, bytes_accessed=4 * count * BLK * width, transcendentals=0),
        name="pick",
    )(index, blocks, valid)


def rms_scale(values):
    return lax.rsqrt(jnp.mean(values * values, axis=1, keepdims=True) + EPSILON)


def rotate(values, cosine, sine):
    half = HD // 2
    first, second = values[:, :half], values[:, half:]
    return jnp.concatenate([first * cosine - second * sine, second * cosine + first * sine], axis=1)


def flip_pairs(array):
    tiles = array.reshape(-1, 2, 2 * BLK, array.shape[1])
    return jnp.stack([tiles[:, 1], tiles[:, 0]], axis=1).reshape(array.shape)


def shards(
    dp_axes,
    tokens,
    cotangent,
    attn_norm,
    w_query,
    w_key,
    w_value,
    w_output,
    mlp_norm,
    w_gate,
    w_up,
    w_down,
    block_counts,
    trims,
    block_order,
):
    rows, width = tokens.shape
    count = rows * TPN
    weight_rows = w_gate.shape[0]
    rank = lax.axis_index(TP_AXES)
    upper = lax.axis_index("zh")
    core = lax.axis_index("c")
    group = lax.axis_index(dp_axes)

    nought = jnp.minimum(block_counts[0, 0], 0).astype(F32)

    counts_row = lax.dynamic_slice_in_dim(block_counts, group, 1, 0)[0]
    trim_row = lax.dynamic_slice_in_dim(trims, group, 1, 0)[0]
    order_row = lax.dynamic_slice_in_dim(block_order, group, 1, 0)[0]
    number = counts_row.shape[0]
    earlier = np.tril(np.ones((number, number), np.int32))
    seq_ends = jnp.sum(jnp.asarray(earlier) * counts_row[None, :], axis=1)
    seq_starts = seq_ends - counts_row
    ranks = rank ^ jnp.arange(TPN, dtype=jnp.int32)
    tiles = upper * TPN + ranks
    index = (tiles[:, None] * rows + jnp.arange(rows, dtype=jnp.int32)[None, :]).reshape(-1)
    block = index // BLK
    inside = (block[:, None] >= seq_starts[None, :]) & (block[:, None] < seq_ends[None, :])
    low = jnp.sum(jnp.where(inside, seq_starts[None, :] * BLK, 0), axis=1)
    limit = jnp.sum(jnp.where(inside, (counts_row * BLK - trim_row)[None, :], 0), axis=1)
    position = index - low
    valid = (position < limit).astype(F32)[:, None]
    high = jnp.minimum(index, low + limit - 1)
    info = jnp.concatenate(
        [
            jnp.stack([rank, upper]).astype(jnp.int32),
            (low.reshape(TPN, rows)[:, 0] // rows).astype(jnp.int32),
        ]
    )
    low, high = low[:, None], high[:, None]
    freqs = jnp.exp(jnp.arange(HD // 2, dtype=F32) * (-2.0 * math.log(THETA) / HD))
    angle = position.astype(F32)[:, None] * freqs[None, :]
    cosine, sine = jnp.cos(angle), jnp.sin(angle)
    is_key = core == 0
    cosine_kv = jnp.where(is_key, cosine, 1.0)
    sine_kv = jnp.where(is_key, sine, 0.0)

    def ranked(weight):
        return weight.reshape(weight_rows, TPN, -1)

    def scaled_by(weight, gain):
        return (weight.astype(F32) * gain.astype(F32)[:, None, None]).astype(BF)

    key_value = jnp.stack(
        [w_key.reshape(weight_rows, TPN // 2, HD), w_value.reshape(weight_rows, TPN // 2, HD)], axis=2
    ).reshape(weight_rows, TPN, HD)
    attn_rows = jnp.concatenate([ranked(w_query), key_value], axis=2)
    in_part = deal_columns(scaled_by(attn_rows, attn_norm))
    slots = order_row.shape[0]
    per_rank = rows // BLK
    slot_ids = jnp.arange(slots, dtype=jnp.int32)
    home = (tiles[:, None] * per_rank + jnp.arange(per_rank, dtype=jnp.int32)[None, :]).reshape(-1)
    slot = jnp.sum(jnp.where(order_row[None, :] == home[:, None], slot_ids[None, :], 0), axis=1)
    owner = slot // per_rank
    pick = (((owner % TPN) ^ rank) * 2 + (owner // TPN ^ upper)) * per_rank + slot % per_rank

    def outer_gather(part, other):
        return gather_some(in_order(part, other, "zh"), dp_axes)

    x_low, in_part = gather_rows(tokens, in_part)
    in_zh = swap(in_part, "zh")
    in_mine, in_other = outer_gather(in_part, in_zh)
    x_all = x_low.astype(F32)
    xn_one = (x_all * rms_scale(x_all)).astype(BF)
    fsdp = dp_axes + ("zh",)
    cot_other = swap(cotangent, "zh")
    w_output, w_gate_late, w_up_late, w_down_late, x_low = meet(w_output, w_gate, w_up, w_down, x_low)
    out_part = deal_columns(ranked(w_output))
    gate_part = deal_columns(scaled_by(ranked(w_gate_late), mlp_norm))
    cot_pair = meet(cotangent, cot_other, in_zh, x_low, gate_part)[:2]
    xn_one, in_other = meet(xn_one, in_other)
    (cot_all,) = gather_rows(jnp.concatenate(cot_pair, axis=0))
    attn_in = in_order(in_mine, in_other, dp_axes[0])
    gate_half = lax.all_gather(gate_part, "zh", axis=0, tiled=True)
    attn_out = lax.all_gather(out_part, fsdp, axis=0, tiled=True)
    up_part = deal_columns(scaled_by(ranked(w_up_late), mlp_norm))
    up_half = lax.all_gather(up_part, "zh", axis=0, tiled=True)
    down_part = deal_columns(ranked(w_down_late))
    projected = dot(xn_one, attn_in, ((1,), (0,)))
    queries = rotate(projected[:, :HD], cosine, sine).astype(BF)
    kv_mine = rotate(projected[:, HD:], cosine_kv, sine_kv).astype(BF)
    kv_lower = lax.ppermute(kv_mine, "zh", [(0, 1)])
    kv_lower, gate_half = meet(kv_lower, gate_half)
    gate_mine, gate_other = gather_some(gate_half, dp_axes)
    kv_all = jnp.concatenate([kv_mine, kv_lower], axis=0)
    kv_other = jnp.concatenate([flip_pairs(swap(kv_mine, "c")), flip_pairs(swap(kv_lower, "c"))], axis=0)
    keys = jnp.where(is_key, kv_all, kv_other)
    values = jnp.where(is_key, kv_other, kv_all)
    attended, lse = attention_forward(info, queries, keys, values, low, high)
    attended, cot_all, gate_other, up_half, down_part = meet(attended, cot_all, gate_other, up_half, down_part)
    down_half = lax.all_gather(down_part, "zh", axis=0, tiled=True)
    up_mine, up_other = gather_some(up_half, dp_axes)
    branch_parts = dot(attended, attn_out, ((1,), (1,)), BF)
    branch_attn = scatter_end(*scatter_begin(core_sum(branch_parts)))
    grad_mlp = pick_blocks(pick.astype(jnp.int32), cot_all, valid)
    branch_attn, grad_mlp, up_other, down_half = meet(branch_attn, grad_mlp, up_other, down_half)
    down_mine, down_other = gather_some(down_half, dp_axes)
    gate_w = in_order(gate_mine, gate_other, dp_axes[0])

    x_own = tokens.astype(F32)
    scale_one = rms_scale(x_own)
    xhat_one = x_own * scale_one
    resid = x_own + branch_attn
    scale_two = rms_scale(resid)
    xhat_two = resid * scale_two
    up_w = in_order(up_mine, up_other, dp_axes[0])
    xn_two, down_other = gather_rows(xhat_two.astype(BF), last=down_other)
    down = in_order(down_mine, down_other, dp_axes[0])

    ff_part = w_gate.shape[1] // TPN
    outer = dp_axes[0]
    hidden, grad_gate_act, grad_up_act, mlp_parts, scaled_parts = feed_forward(xn_two, grad_mlp, gate_w, up_w, down)

    def rest(got, keep):
        mine = add_up(got, keep)
        for axis in dp_axes[1:]:
            mine = add_up(*halve(mine, axis))
        return halve(mine, "zh")

    got_first, got_second, *kept = scatter_begin(core_sum(scaled_parts))
    down_got, down_keep = halve(dot(grad_mlp, hidden, ((0,), (0,)), BF), outer)
    gate_got, gate_keep = halve(dot(xn_two, grad_gate_act, ((0,), (0,)), BF), outer)
    up_grad = dot(xn_two, grad_up_act, ((0,), (0,)), BF)
    got_first, got_second, down_got = meet(got_first, got_second, down_got)
    down_got, down_keep = rest(down_got, down_keep)
    scaled = scatter_end(got_first, got_second, *kept)
    scaled, gate_keep, up_grad = meet(scaled, gate_keep, up_grad)

    grad_final = grad_mlp[:rows].astype(F32)
    grad_resid = grad_final + scale_two * (
        scaled - xhat_two * jnp.mean(scaled * xhat_two, axis=1, keepdims=True)
    )


    grad_low = grad_resid.astype(BF)
    grad_branch, down_got, gate_got = gather_rows(grad_low, down_got, last=gate_got)
    mlp_sums, grad_branch = meet(core_sum(mlp_parts), grad_branch)
    begun = scatter_begin(mlp_sums)
    gate_got, gate_keep = rest(gate_got, gate_keep)
    up_got, up_keep = halve(up_grad, outer)
    grad_attn_f32 = dot(grad_branch, attn_out, ((1,), (0,)))
    grad_attn, keep_first, keep_second = meet(grad_attn_f32.astype(BF), *begun[2:])
    begun = (*begun[:2], keep_first, keep_second)
    delta = jnp.sum(grad_attn.astype(F32) * attended.astype(F32), axis=1, keepdims=True)
    grad_q, grad_k, grad_v = attention_backward(
        info, queries, keys, values, low, high, lse, delta, grad_attn
    )
    grad_q, grad_k, grad_v, gate_got, *begun = meet(grad_q, grad_k, grad_v, gate_got, *begun)
    send = jnp.where(is_key, grad_v, grad_k).astype(BF)
    keep = jnp.where(is_key, grad_k, grad_v)
    chip = keep + flip_pairs(swap(send, "c")).astype(F32)
    from_upper = lax.ppermute(chip[count:].astype(BF), "zh", [(1, 0)])
    branch_mlp = scatter_end(*begun)
    grad_down_w = deal_rows(after(add_up(down_got, down_keep), chip, nought))
    from_upper, up_got, branch_mlp = meet(from_upper, up_got, branch_mlp)
    up_got, up_keep = rest(up_got, up_keep)
    final = resid + branch_mlp
    output = final.astype(BF)
    valid_own = valid[:rows]
    squares = [jnp.sum(a * a * valid_own, axis=0) for a in (branch_attn, resid, branch_mlp, final)]
    square_cols = jnp.pad(jnp.stack(squares, axis=1), ((0, 0), (0, BLK - len(squares)))).astype(BF)
    grad_out = jnp.concatenate([dot(grad_branch, attended, ((0,), (0,)), BF), square_cols], axis=1)
    out_got, out_keep = halve(grad_out, outer)
    grad_kv = chip[:count] + from_upper.astype(F32)
    grad_q_proj = rotate(grad_q, cosine, -sine).astype(BF)
    grad_kv_proj = rotate(grad_kv, cosine_kv, -sine_kv).astype(BF)
    grad_proj = jnp.concatenate([grad_q_proj, grad_kv_proj], axis=1)
    grad_xn_one_parts = dot(grad_proj, attn_in, ((1,), (1,)), BF)
    grad_xn_one_parts, grad_proj, out_got, grad_down_w = meet(grad_xn_one_parts, grad_proj, out_got, grad_down_w)
    out_got, out_keep = rest(out_got, out_keep)
    in_got, in_keep = halve(dot(xn_one, grad_proj, ((0,), (0,)), BF), outer)
    got_first, got_second, *kept = scatter_begin(core_sum(grad_xn_one_parts))
    grad_gate_w = deal_rows(after(add_up(gate_got, gate_keep), kept[0], nought))
    got_first, got_second, up_got, in_got = meet(got_first, got_second, up_got, in_got)
    in_got, in_keep = rest(in_got, in_keep)
    scaled = scatter_end(got_first, got_second, *kept)
    scaled, out_got = meet(scaled, out_got)
    input_grad = grad_resid + scale_one * (
        scaled - xhat_one * jnp.mean(scaled * xhat_one, axis=1, keepdims=True)
    )
    grad_up_w = deal_rows(add_up(up_got, up_keep))
    late = jnp.concatenate([add_up(out_got, out_keep), add_up(in_got, in_keep)], axis=1)
    late_w = deal_rows(late)
    grad_out_w, grad_in_w = late_w[:, :, : HD + BLK], late_w[:, :, HD + BLK :]
    square_sums = jnp.sum(grad_out_w[:, :, HD : HD + 4], axis=1)
    grad_out_w = grad_out_w[:, :, :HD]

    def gain_gradient(*pairs):
        return sum(jnp.sum(ranked(w).astype(F32) * g, axis=(1, 2)) for w, g in pairs)

    grad_attn_norm = gain_gradient((attn_rows, grad_in_w))
    grad_mlp_norm = gain_gradient((w_gate, grad_gate_w), (w_up, grad_up_w))
    gain_one, gain_two = (g.astype(F32)[:, None, None] for g in (attn_norm, mlp_norm))
    grad_in_w, grad_gate_w, grad_up_w = grad_in_w * gain_one, grad_gate_w * gain_two, grad_up_w * gain_two

    valid_count = jnp.sum((block_counts * BLK - trims).astype(F32))
    rms_stats = jnp.sqrt(square_sums / valid_count).T

    def flat(array):
        return array.reshape(weight_rows, -1)

    grad_kv_w = grad_in_w[:, :, HD:].reshape(weight_rows, TPN // 2, 2, HD)
    return (
        output,
        input_grad.astype(BF),
        grad_attn_norm,
        flat(grad_in_w[:, :, :HD]),
        flat(grad_kv_w[:, :, 0]),
        flat(grad_kv_w[:, :, 1]),
        flat(grad_out_w),
        grad_mlp_norm,
        flat(grad_gate_w),
        flat(grad_up_w),
        flat(grad_down_w),
        rms_stats,
    )


def solution(mesh):
    outer = mesh.shape["dp"]
    bits = outer.bit_length() - 1
    dp_axes = tuple(f"x{i}" for i in range(bits))
    names = dp_axes + ("zh",) + TP_AXES
    fine = Mesh(mesh.devices.reshape((2,) * len(names)), names)
    rows, flat = P(names, None), P(names)
    in_specs = (rows, rows, flat, rows, rows, rows, rows, flat, rows, rows, rows, P(), P(), P())
    out_specs = (rows, rows, flat, rows, rows, rows, rows, flat, rows, rows, rows, P(None, names))
    return jax.shard_map(
        functools.partial(shards, dp_axes),
        mesh=fine,
        in_specs=in_specs,
        out_specs=out_specs,
        check_vma=False,
    )
```

```python
import functools
import math

import jax
import jax.numpy as jnp
import numpy as np
from jax import lax
from jax.experimental import pallas as pl
from jax.experimental.pallas import tpu as pltpu
from jax.sharding import Mesh
from jax.sharding import PartitionSpec as P

HD = 256
BLK = 128
EPSILON = 1e-06
THETA = 1000042.0
TP_AXES = ("zl", "y", "c")
TPN = 8
NEG = -1e30
BF = jnp.bfloat16
F32 = jnp.float32


def swap(array, axis):
    return lax.ppermute(array, axis, [(0, 1), (1, 0)])


def dot(left, right, contract, out=F32):
    got = lax.dot_general(left, right, (contract, ((), ())), preferred_element_type=F32)
    return got.astype(out)


def meet(*arrays):
    return lax.optimization_barrier(arrays)


def after(array, token, nought):
    last = token[(slice(-1, None),) * token.ndim].astype(F32) * nought
    return array + last.reshape((1,) * array.ndim).astype(array.dtype)


def gather_rows(own, *others, last=None):
    rows = own.shape[0]
    half = rows // 2
    first, second = own[:half], own[half:]
    first_y = swap(first, "y")
    second_z = swap(second, "zl")
    core_own = swap(own, "c")
    if others:
        first_y, second_z, *others = meet(first_y, second_z, *others)
    core_one = swap(jnp.stack([first_y, second_z]), "c")
    first_z = swap(jnp.stack([first, first_y]), "zl")
    second_y = swap(jnp.stack([second, second_z]), "y")
    if last is not None:
        first_z, second_y, last = meet(first_z, second_y, last)
        others = (*others, last)
    core_two = swap(jnp.concatenate([first_z, second_y]), "c")
    pieces = [
        own,
        core_own,
        first_y,
        second_y[0],
        core_one[0],
        core_two[2],
        first_z[0],
        second_z,
        core_two[0],
        core_one[1],
        first_z[1],
        second_y[1],
        core_two[1],
        core_two[3],
    ]
    whole = jnp.concatenate(pieces, axis=0).reshape(TPN * rows, own.shape[1])
    return (whole, *others)


def core_sum(parts):
    parts = parts.reshape(TPN, -1, parts.shape[1])
    return parts[0::2].astype(F32) + swap(parts[1::2], "c").astype(F32)


def scatter_begin(total):
    half = total.shape[1] // 2
    first, second = total[:, :half], total[:, half:]
    got_first = swap(first[1::2].astype(BF), "y")
    got_second = swap(second[2:].astype(BF), "zl")
    return got_first, got_second, first[0::2], second[:2]


def scatter_end(got_first, got_second, first, second):
    first = first + got_first.astype(F32)
    second = second + got_second.astype(F32)
    got_first = swap(first[1].astype(BF), "zl").astype(F32)
    got_second = swap(second[1].astype(BF), "y").astype(F32)
    return jnp.concatenate([first[0] + got_first, second[0] + got_second], axis=0)


def deal_columns(piece):
    rows, _, columns = piece.shape
    return lax.all_to_all(piece, TP_AXES, 1, 0, tiled=True).reshape(rows * TPN, columns)


def in_order(mine, other, axis):
    low = lax.axis_index(axis) == 0
    return jnp.concatenate([jnp.where(low, mine, other), jnp.where(low, other, mine)], axis=0)


def gather_some(mine, axes):
    for axis in axes[:0:-1]:
        mine = in_order(mine, swap(mine, axis), axis)
    return mine, swap(mine, axes[0])


def halve(partial, axis):
    half = partial.shape[0] // 2
    place = lax.axis_index(axis)
    send = lax.dynamic_slice_in_dim(partial, (1 - place) * half, half, 0).astype(BF)
    keep = lax.dynamic_slice_in_dim(partial, place * half, half, 0)
    return swap(send, axis), keep


def add_up(got, keep):
    return keep.astype(F32) + got.astype(F32)


def deal_rows(mine):
    rows = mine.shape[0] // TPN
    low = mine.astype(BF).reshape(TPN, rows, mine.shape[1])
    got = lax.all_to_all(low, TP_AXES, 0, 0, tiled=True)
    return jnp.swapaxes(got, 0, 1).astype(F32)


def slot_of(tile, info):
    return ((tile // TPN) ^ info[1]) * TPN + ((tile % TPN) ^ info[0])


def forward_kernel(info, q_ref, k_ref, v_ref, lo_ref, hi_ref, out_ref, lse_ref, top, total, acc):
    step = pl.program_id(0)
    rows = q_ref.shape[0]
    last = info[1] * TPN + (info[0] ^ step)
    queries = q_ref[...]
    low, high = lo_ref[...], hi_ref[...]
    top[...] = jnp.full_like(top, NEG)
    total[...] = jnp.zeros_like(total)
    acc[...] = jnp.zeros_like(acc)

    def body(tile, carry):
        start = pl.multiple_of(slot_of(tile, info) * rows, rows)
        keys = k_ref[pl.ds(start, rows), :]
        values = v_ref[pl.ds(start, rows), :]
        scores = dot(queries, keys, ((1,), (1,))) * (HD**-0.5)
        place = tile * rows + lax.broadcasted_iota(jnp.int32, scores.shape, 1)
        scores = jnp.where((place >= low) & (place <= high), scores, NEG)
        before = top[...]
        now = jnp.maximum(before, jnp.max(scores, axis=1, keepdims=True))
        prob = jnp.exp(scores - now)
        fade = jnp.exp(before - now)
        top[...] = now
        total[...] = total[...] * fade + jnp.sum(prob, axis=1, keepdims=True)
        acc[...] = acc[...] * fade + dot(prob.astype(BF), values, ((1,), (0,)))
        return carry

    lax.fori_loop(info[2 + step], last + 1, body, 0)
    out_ref[...] = (acc[...] / total[...]).astype(BF)
    lse_ref[...] = top[...] + jnp.log(total[...])


def backward_kernel(
    info, q_ref, k_ref, v_ref, lo_ref, hi_ref, lse_ref, delta_ref, grad_ref, gq_ref, gk_ref, gv_ref, acc
):
    step = pl.program_id(0)
    rows = q_ref.shape[0]
    last = info[1] * TPN + (info[0] ^ step)
    queries, grads = q_ref[...], grad_ref[...]
    low, high = lo_ref[...], hi_ref[...]
    lse, delta = lse_ref[...], delta_ref[...]
    acc[...] = jnp.zeros_like(acc)

    @pl.when(step == 0)
    def _():
        gk_ref[...] = jnp.zeros_like(gk_ref)
        gv_ref[...] = jnp.zeros_like(gv_ref)

    def body(tile, carry):
        start = pl.multiple_of(slot_of(tile, info) * rows, rows)
        keys = k_ref[pl.ds(start, rows), :]
        values = v_ref[pl.ds(start, rows), :]
        scores = dot(queries, keys, ((1,), (1,))) * (HD**-0.5)
        place = tile * rows + lax.broadcasted_iota(jnp.int32, scores.shape, 1)
        scores = jnp.where((place >= low) & (place <= high), scores, NEG)
        prob = jnp.exp(scores - lse)
        dprob = dot(grads, values, ((1,), (1,)))
        dscore = (prob * (dprob - delta)).astype(BF)
        acc[...] += dot(dscore, keys, ((1,), (0,)))
        gk_ref[pl.ds(start, rows), :] += dot(dscore, queries, ((0,), (0,))) * (HD**-0.5)
        gv_ref[pl.ds(start, rows), :] += dot(prob.astype(BF), grads, ((0,), (0,)))
        return carry

    lax.fori_loop(info[2 + step], last + 1, body, 0)
    gq_ref[...] = acc[...] * (HD**-0.5)


def tile_spec(rows, width):
    return pl.BlockSpec((rows, width), lambda i, info: (i, 0))


def whole_spec(rows, width):
    return pl.BlockSpec((rows, width), lambda i, info: (0, 0))


def attention_forward(info, queries, keys, values, low, high):
    count, rows = queries.shape[0], queries.shape[0] // TPN
    span = keys.shape[0]
    return pl.pallas_call(
        forward_kernel,
        grid_spec=pltpu.PrefetchScalarGridSpec(
            num_scalar_prefetch=1,
            grid=(TPN,),
            in_specs=[
                tile_spec(rows, HD),
                whole_spec(span, HD),
                whole_spec(span, HD),
                tile_spec(rows, 1),
                tile_spec(rows, 1),
            ],
            out_specs=[tile_spec(rows, HD), tile_spec(rows, 1)],
            scratch_shapes=[
                pltpu.VMEM((rows, 1), F32),
                pltpu.VMEM((rows, 1), F32),
                pltpu.VMEM((rows, HD), F32),
            ],
        ),
        out_shape=[
            jax.ShapeDtypeStruct((count, HD), BF),
            jax.ShapeDtypeStruct((count, 1), F32),
        ],
        compiler_params=pltpu.CompilerParams(vmem_limit_bytes=40 << 20),
        cost_estimate=pl.CostEstimate(
            flops=4 * count * count * HD, bytes_accessed=8 << 20, transcendentals=count * count
        ),
        name="attend",
    )(info, queries, keys, values, low, high)


def attention_backward(info, queries, keys, values, low, high, lse, delta, grads):
    count, rows = queries.shape[0], queries.shape[0] // TPN
    span = keys.shape[0]
    return pl.pallas_call(
        backward_kernel,
        grid_spec=pltpu.PrefetchScalarGridSpec(
            num_scalar_prefetch=1,
            grid=(TPN,),
            in_specs=[
                tile_spec(rows, HD),
                whole_spec(span, HD),
                whole_spec(span, HD),
                tile_spec(rows, 1),
                tile_spec(rows, 1),
                tile_spec(rows, 1),
                tile_spec(rows, 1),
                tile_spec(rows, HD),
            ],
            out_specs=[tile_spec(rows, HD), whole_spec(span, HD), whole_spec(span, HD)],
            scratch_shapes=[pltpu.VMEM((rows, HD), F32)],
        ),
        out_shape=[
            jax.ShapeDtypeStruct((count, HD), F32),
            jax.ShapeDtypeStruct((span, HD), F32),
            jax.ShapeDtypeStruct((span, HD), F32),
        ],
        compiler_params=pltpu.CompilerParams(vmem_limit_bytes=48 << 20),
        cost_estimate=pl.CostEstimate(
            flops=10 * count * count * HD, bytes_accessed=16 << 20, transcendentals=count * count
        ),
        name="attend_back",
    )(info, queries, keys, values, low, high, lse, delta, grads)


def mlp_kernel(x_ref, cot_ref, wg_ref, wu_ref, wd_ref, hidden_ref, gate_ref, up_ref, out_ref, back_ref):
    gate = dot(x_ref[...], wg_ref[...], ((1,), (0,)))
    up = dot(x_ref[...], wu_ref[...], ((1,), (0,)))
    sigma = jax.nn.sigmoid(gate)
    activated = gate * sigma
    hidden = (activated * up).astype(BF)
    hidden_ref[...] = hidden
    grad = dot(cot_ref[...], wd_ref[...], ((1,), (0,)))
    up_act = (grad * activated).astype(BF)
    gate_act = (grad * up * sigma * (1.0 + gate * (1.0 - sigma))).astype(BF)
    gate_ref[...], up_ref[...] = gate_act, up_act
    out_ref[...] = dot(hidden, wd_ref[...], ((1,), (1,)), BF)
    back = dot(gate_act, wg_ref[...], ((1,), (1,))) + dot(up_act, wu_ref[...], ((1,), (1,)))
    back_ref[...] = back.astype(BF)


def feed_forward(normed, cotangent, w_gate, w_up, w_down):
    count, width = normed.shape
    part = w_gate.shape[1]
    rows = count // TPN
    wide = pl.BlockSpec((rows, width), lambda i: (i, 0))
    narrow = pl.BlockSpec((rows, part), lambda i: (i, 0))
    weight = pl.BlockSpec((width, part), lambda i: (0, 0), pipeline_mode=pl.Buffered(1))
    return pl.pallas_call(
        mlp_kernel,
        grid=(TPN,),
        in_specs=[wide, wide, weight, weight, weight],
        out_specs=[narrow, narrow, narrow, wide, wide],
        out_shape=[jax.ShapeDtypeStruct((count, part), BF)] * 3 + [jax.ShapeDtypeStruct((count, width), BF)] * 2,
        compiler_params=pltpu.CompilerParams(vmem_limit_bytes=56 << 20),
        cost_estimate=pl.CostEstimate(
            flops=12 * count * width * part, bytes_accessed=60 << 20, transcendentals=count * part
        ),
        name="mlp",
    )(normed, cotangent, w_gate, w_up, w_down)


def pick_kernel(index, block_ref, valid_ref, out_ref):
    out_ref[...] = block_ref[...] * valid_ref[...].astype(BF)


def pick_blocks(index, blocks, valid):
    count, width = index.shape[0], blocks.shape[1]
    return pl.pallas_call(
        pick_kernel,
        grid_spec=pltpu.PrefetchScalarGridSpec(
            num_scalar_prefetch=1,
            grid=(count,),
            in_specs=[
                pl.BlockSpec((BLK, width), lambda i, index: (index[i], 0)),
                pl.BlockSpec((BLK, 1), lambda i, index: (i, 0)),
            ],
            out_specs=pl.BlockSpec((BLK, width), lambda i, index: (i, 0)),
        ),
        out_shape=jax.ShapeDtypeStruct((count * BLK, width), BF),
        cost_estimate=pl.CostEstimate(flops=0, bytes_accessed=4 * count * BLK * width, transcendentals=0),
        name="pick",
    )(index, blocks, valid)


def rms_scale(values):
    return lax.rsqrt(jnp.mean(values * values, axis=1, keepdims=True) + EPSILON)


def rotate(values, cosine, sine):
    half = HD // 2
    first, second = values[:, :half], values[:, half:]
    return jnp.concatenate([first * cosine - second * sine, second * cosine + first * sine], axis=1)


def flip_pairs(array):
    tiles = array.reshape(-1, 2, 2 * BLK, array.shape[1])
    return jnp.stack([tiles[:, 1], tiles[:, 0]], axis=1).reshape(array.shape)


def shards(
    dp_axes,
    tokens,
    cotangent,
    attn_norm,
    w_query,
    w_key,
    w_value,
    w_output,
    mlp_norm,
    w_gate,
    w_up,
    w_down,
    block_counts,
    trims,
    block_order,
):
    rows, width = tokens.shape
    count = rows * TPN
    weight_rows = w_gate.shape[0]
    rank = lax.axis_index(TP_AXES)
    upper = lax.axis_index("zh")
    core = lax.axis_index("c")
    group = lax.axis_index(dp_axes)

    nought = jnp.minimum(block_counts[0, 0], 0).astype(F32)

    counts_row = lax.dynamic_slice_in_dim(block_counts, group, 1, 0)[0]
    trim_row = lax.dynamic_slice_in_dim(trims, group, 1, 0)[0]
    order_row = lax.dynamic_slice_in_dim(block_order, group, 1, 0)[0]
    number = counts_row.shape[0]
    earlier = np.tril(np.ones((number, number), np.int32))
    seq_ends = jnp.sum(jnp.asarray(earlier) * counts_row[None, :], axis=1)
    seq_starts = seq_ends - counts_row
    ranks = rank ^ jnp.arange(TPN, dtype=jnp.int32)
    tiles = upper * TPN + ranks
    index = (tiles[:, None] * rows + jnp.arange(rows, dtype=jnp.int32)[None, :]).reshape(-1)
    block = index // BLK
    inside = (block[:, None] >= seq_starts[None, :]) & (block[:, None] < seq_ends[None, :])
    low = jnp.sum(jnp.where(inside, seq_starts[None, :] * BLK, 0), axis=1)
    limit = jnp.sum(jnp.where(inside, (counts_row * BLK - trim_row)[None, :], 0), axis=1)
    position = index - low
    valid = (position < limit).astype(F32)[:, None]
    high = jnp.minimum(index, low + limit - 1)
    info = jnp.concatenate(
        [
            jnp.stack([rank, upper]).astype(jnp.int32),
            (low.reshape(TPN, rows)[:, 0] // rows).astype(jnp.int32),
        ]
    )
    low, high = low[:, None], high[:, None]
    freqs = jnp.exp(jnp.arange(HD // 2, dtype=F32) * (-2.0 * math.log(THETA) / HD))
    angle = position.astype(F32)[:, None] * freqs[None, :]
    cosine, sine = jnp.cos(angle), jnp.sin(angle)
    is_key = core == 0
    cosine_kv = jnp.where(is_key, cosine, 1.0)
    sine_kv = jnp.where(is_key, sine, 0.0)

    def ranked(weight):
        return weight.reshape(weight_rows, TPN, -1)

    def scaled_by(weight, gain):
        return (weight.astype(F32) * gain.astype(F32)[:, None, None]).astype(BF)

    key_value = jnp.stack(
        [w_key.reshape(weight_rows, TPN // 2, HD), w_value.reshape(weight_rows, TPN // 2, HD)], axis=2
    ).reshape(weight_rows, TPN, HD)
    attn_rows = jnp.concatenate([ranked(w_query), key_value], axis=2)
    in_part = deal_columns(scaled_by(attn_rows, attn_norm))
    slots = order_row.shape[0]
    per_rank = rows // BLK
    slot_ids = jnp.arange(slots, dtype=jnp.int32)
    home = (tiles[:, None] * per_rank + jnp.arange(per_rank, dtype=jnp.int32)[None, :]).reshape(-1)
    slot = jnp.sum(jnp.where(order_row[None, :] == home[:, None], slot_ids[None, :], 0), axis=1)
    owner = slot // per_rank
    pick = (((owner % TPN) ^ rank) * 2 + (owner // TPN ^ upper)) * per_rank + slot % per_rank

    def outer_gather(part, other):
        return gather_some(in_order(part, other, "zh"), dp_axes)

    x_low, in_part = gather_rows(tokens, in_part)
    in_zh = swap(in_part, "zh")
    in_mine, in_other = outer_gather(in_part, in_zh)
    x_all = x_low.astype(F32)
    xn_one = (x_all * rms_scale(x_all)).astype(BF)
    fsdp = dp_axes + ("zh",)
    cot_other = swap(cotangent, "zh")
    w_output, w_gate_late, w_up_late, w_down_late, x_low = meet(w_output, w_gate, w_up, w_down, x_low)
    out_part = deal_columns(ranked(w_output))
    gate_part = deal_columns(scaled_by(ranked(w_gate_late), mlp_norm))
    cot_pair = meet(cotangent, cot_other, in_zh, x_low, gate_part)[:2]
    xn_one, in_other = meet(xn_one, in_other)
    (cot_all,) = gather_rows(jnp.concatenate(cot_pair, axis=0))
    attn_in = in_order(in_mine, in_other, dp_axes[0])
    gate_half = lax.all_gather(gate_part, "zh", axis=0, tiled=True)
    attn_out = lax.all_gather(out_part, fsdp, axis=0, tiled=True)
    up_part = deal_columns(scaled_by(ranked(w_up_late), mlp_norm))
    up_half = lax.all_gather(up_part, "zh", axis=0, tiled=True)
    down_part = deal_columns(ranked(w_down_late))
    projected = dot(xn_one, attn_in, ((1,), (0,)))
    queries = rotate(projected[:, :HD], cosine, sine).astype(BF)
    kv_mine = rotate(projected[:, HD:], cosine_kv, sine_kv).astype(BF)
    kv_lower = lax.ppermute(kv_mine, "zh", [(0, 1)])
    kv_lower, gate_half = meet(kv_lower, gate_half)
    gate_mine, gate_other = gather_some(gate_half, dp_axes)
    kv_all = jnp.concatenate([kv_mine, kv_lower], axis=0)
    kv_other = jnp.concatenate([flip_pairs(swap(kv_mine, "c")), flip_pairs(swap(kv_lower, "c"))], axis=0)
    keys = jnp.where(is_key, kv_all, kv_other)
    values = jnp.where(is_key, kv_other, kv_all)
    attended, lse = attention_forward(info, queries, keys, values, low, high)
    attended, cot_all, gate_other, up_half, down_part = meet(attended, cot_all, gate_other, up_half, down_part)
    down_half = lax.all_gather(down_part, "zh", axis=0, tiled=True)
    up_mine, up_other = gather_some(up_half, dp_axes)
    branch_parts = dot(attended, attn_out, ((1,), (1,)), BF)
    branch_attn = scatter_end(*scatter_begin(core_sum(branch_parts)))
    grad_mlp = pick_blocks(pick.astype(jnp.int32), cot_all, valid)
    branch_attn, grad_mlp, up_other, down_half = meet(branch_attn, grad_mlp, up_other, down_half)
    down_mine, down_other = gather_some(down_half, dp_axes)
    gate_w = in_order(gate_mine, gate_other, dp_axes[0])

    x_own = tokens.astype(F32)
    scale_one = rms_scale(x_own)
    xhat_one = x_own * scale_one
    resid = x_own + branch_attn
    scale_two = rms_scale(resid)
    xhat_two = resid * scale_two
    up_w = in_order(up_mine, up_other, dp_axes[0])
    xn_two, down_other = gather_rows(xhat_two.astype(BF), last=down_other)
    down = in_order(down_mine, down_other, dp_axes[0])

    ff_part = w_gate.shape[1] // TPN
    outer = dp_axes[0]
    hidden, grad_gate_act, grad_up_act, mlp_parts, scaled_parts = feed_forward(xn_two, grad_mlp, gate_w, up_w, down)

    def rest(got, keep):
        mine = add_up(got, keep)
        for axis in dp_axes[1:]:
            mine = add_up(*halve(mine, axis))
        return halve(mine, "zh")

    got_first, got_second, *kept = scatter_begin(core_sum(scaled_parts))
    down_got, down_keep = halve(dot(grad_mlp, hidden, ((0,), (0,)), BF), outer)
    gate_got, gate_keep = halve(dot(xn_two, grad_gate_act, ((0,), (0,)), BF), outer)
    up_grad = dot(xn_two, grad_up_act, ((0,), (0,)), BF)
    got_first, got_second, down_got = meet(got_first, got_second, down_got)
    down_got, down_keep = rest(down_got, down_keep)
    scaled = scatter_end(got_first, got_second, *kept)
    scaled, gate_keep, up_grad = meet(scaled, gate_keep, up_grad)

    grad_final = grad_mlp[:rows].astype(F32)
    grad_resid = grad_final + scale_two * (
        scaled - xhat_two * jnp.mean(scaled * xhat_two, axis=1, keepdims=True)
    )


    grad_low = grad_resid.astype(BF)
    grad_branch, down_got, gate_got = gather_rows(grad_low, down_got, last=gate_got)
    mlp_sums, grad_branch = meet(core_sum(mlp_parts), grad_branch)
    begun = scatter_begin(mlp_sums)
    gate_got, gate_keep = rest(gate_got, gate_keep)
    up_got, up_keep = halve(up_grad, outer)
    grad_attn_f32 = dot(grad_branch, attn_out, ((1,), (0,)))
    grad_attn, keep_first, keep_second = meet(grad_attn_f32.astype(BF), *begun[2:])
    begun = (*begun[:2], keep_first, keep_second)
    delta = jnp.sum(grad_attn.astype(F32) * attended.astype(F32), axis=1, keepdims=True)
    grad_q, grad_k, grad_v = attention_backward(
        info, queries, keys, values, low, high, lse, delta, grad_attn
    )
    grad_q, grad_k, grad_v, gate_got, *begun = meet(grad_q, grad_k, grad_v, gate_got, *begun)
    send = jnp.where(is_key, grad_v, grad_k).astype(BF)
    keep = jnp.where(is_key, grad_k, grad_v)
    chip = keep + flip_pairs(swap(send, "c")).astype(F32)
    from_upper = lax.ppermute(chip[count:].astype(BF), "zh", [(1, 0)])
    branch_mlp = scatter_end(*begun)
    early = jnp.concatenate([add_up(down_got, down_keep), add_up(gate_got, gate_keep)], axis=1)
    early_w = deal_rows(after(early, chip, nought))
    from_upper, up_got, branch_mlp = meet(from_upper, up_got, branch_mlp)
    up_got, up_keep = rest(up_got, up_keep)
    final = resid + branch_mlp
    output = final.astype(BF)
    valid_own = valid[:rows]
    squares = [jnp.sum(a * a * valid_own, axis=0) for a in (branch_attn, resid, branch_mlp, final)]
    square_cols = jnp.pad(jnp.stack(squares, axis=1), ((0, 0), (0, BLK - len(squares)))).astype(BF)
    grad_out = jnp.concatenate([dot(grad_branch, attended, ((0,), (0,)), BF), square_cols], axis=1)
    out_got, out_keep = halve(grad_out, outer)
    grad_kv = chip[:count] + from_upper.astype(F32)
    grad_q_proj = rotate(grad_q, cosine, -sine).astype(BF)
    grad_kv_proj = rotate(grad_kv, cosine_kv, -sine_kv).astype(BF)
    grad_proj = jnp.concatenate([grad_q_proj, grad_kv_proj], axis=1)
    grad_xn_one_parts = dot(grad_proj, attn_in, ((1,), (1,)), BF)
    grad_xn_one_parts, grad_proj, out_got, early_w = meet(grad_xn_one_parts, grad_proj, out_got, early_w)
    grad_down_w, grad_gate_w = early_w[:, :, :ff_part], early_w[:, :, ff_part:]
    out_got, out_keep = rest(out_got, out_keep)
    in_got, in_keep = halve(dot(xn_one, grad_proj, ((0,), (0,)), BF), outer)
    got_first, got_second, *kept = scatter_begin(core_sum(grad_xn_one_parts))
    got_first, got_second, up_got, in_got = meet(got_first, got_second, up_got, in_got)
    in_got, in_keep = rest(in_got, in_keep)
    scaled = scatter_end(got_first, got_second, *kept)
    scaled, out_got, in_got = meet(scaled, out_got, in_got)
    input_grad = grad_resid + scale_one * (
        scaled - xhat_one * jnp.mean(scaled * xhat_one, axis=1, keepdims=True)
    )
    grad_up_w = deal_rows(add_up(up_got, up_keep))
    late = jnp.concatenate([add_up(out_got, out_keep), add_up(in_got, in_keep)], axis=1)
    late_w = deal_rows(late)
    grad_out_w, grad_in_w = late_w[:, :, : HD + BLK], late_w[:, :, HD + BLK :]
    square_sums = jnp.sum(grad_out_w[:, :, HD : HD + 4], axis=1)
    grad_out_w = grad_out_w[:, :, :HD]

    def gain_gradient(*pairs):
        return sum(jnp.sum(ranked(w).astype(F32) * g, axis=(1, 2)) for w, g in pairs)

    grad_attn_norm = gain_gradient((attn_rows, grad_in_w))
    grad_mlp_norm = gain_gradient((w_gate, grad_gate_w), (w_up, grad_up_w))
    gain_one, gain_two = (g.astype(F32)[:, None, None] for g in (attn_norm, mlp_norm))
    grad_in_w, grad_gate_w, grad_up_w = grad_in_w * gain_one, grad_gate_w * gain_two, grad_up_w * gain_two

    valid_count = jnp.sum((block_counts * BLK - trims).astype(F32))
    rms_stats = jnp.sqrt(square_sums / valid_count).T

    def flat(array):
        return array.reshape(weight_rows, -1)

    grad_kv_w = grad_in_w[:, :, HD:].reshape(weight_rows, TPN // 2, 2, HD)
    return (
        output,
        input_grad.astype(BF),
        grad_attn_norm,
        flat(grad_in_w[:, :, :HD]),
        flat(grad_kv_w[:, :, 0]),
        flat(grad_kv_w[:, :, 1]),
        flat(grad_out_w),
        grad_mlp_norm,
        flat(grad_gate_w),
        flat(grad_up_w),
        flat(grad_down_w),
        rms_stats,
    )


def solution(mesh):
    outer = mesh.shape["dp"]
    bits = outer.bit_length() - 1
    dp_axes = tuple(f"x{i}" for i in range(bits))
    names = dp_axes + ("zh",) + TP_AXES
    fine = Mesh(mesh.devices.reshape((2,) * len(names)), names)
    rows, flat = P(names, None), P(names)
    in_specs = (rows, rows, flat, rows, rows, rows, rows, flat, rows, rows, rows, P(), P(), P())
    out_specs = (rows, rows, flat, rows, rows, rows, rows, flat, rows, rows, rows, P(None, names))
    return jax.shard_map(
        functools.partial(shards, dp_axes),
        mesh=fine,
        in_specs=in_specs,
        out_specs=out_specs,
        check_vma=False,
    )
```
